128 devices in a mesh: leaf: 128 (over y, z, x, core).
Axes of the slice: x: 4, y: 4, z: 4, core: 2. Of those that a mesh axis runs over, the one named last changes fastest.
Arguments:
- points: bfloat16 [64, 131072], P(None, 'leaf'), may hold values from -6 to 6
- weights: bfloat16 [131072, 512], P('leaf'), may hold values from -1.1953125 to 1.1953125
- interp: bfloat16 [131072, 512], P('leaf'), may hold values from -0.1875 to 0.1875
- transfers: bfloat16 [128, 5, 512, 512], P('leaf'), may hold values from -0.25 to 0.25
- near_mask: int32 [128, 4], P('leaf'), may hold values 0 or 1
- skel_index: int32 [128, 512], P('leaf'), may hold values from 0 to 1023, as said below
Outputs:
- product: bfloat16 [131072, 512], P('leaf')
The draws below stay inside these ranges and needn't reach their ends.
Inputs may be any that keep to these rules, and one draw needn't show every extreme that they name: `skel_index`: each row holds 512 distinct ranks.
All inputs are finite; a program needn't handle non-finite values. No bound on the sum of `near_mask` on one device may be relied on, other than what follows from the above.
Results may differ from the reference program's by a relative error of at most 0.0075.
Values may be sent and summed in bfloat16 or wider, within the bound.
No kernel may reach another device: no remote copies, remote signals or barrier semaphores. Data moves between devices by JAX's collectives and lax.ppermute only.
A program may use at most 128 MiB of HBM per device.

```python
import jax
import jax.numpy as jnp
from jax import lax

DIM = 64
RHS = 512
S = 512
NPTS = 1024
LEVELS = 5
RADIUS = 2
LEAVES = 128
POINTS = 131072


def pick_row(row_key):
    return jax.random.permutation(row_key, NPTS)[:S]


def draw_skel_index(key, part):
    row_keys = jax.random.split(jax.random.fold_in(key, 17), LEAVES)
    return jax.vmap(pick_row)(row_keys).astype(jnp.int32)


def set_ends(array, stream_key, low, largest):
    index_at = [jax.random.randint(jax.random.fold_in(stream_key, axis), (), 0, length) for axis, length in enumerate(array.shape)]
    widest = array.shape.index(max(array.shape))
    next_to = index_at[:widest] + [(index_at[widest] + 1) % array.shape[widest]] + index_at[widest + 1:]
    return array.at[tuple(index_at)].set(low).at[tuple(next_to)].set(largest)


def levels(stream_key, extent, shards, smallest, top_value):
    def one(axis_at, parts):
        steps = jax.random.uniform(jax.random.fold_in(jax.random.fold_in(stream_key, 6), axis_at), (parts,), jnp.float32, smallest / len(shards), top_value / len(shards))
        return jnp.repeat(jnp.exp(steps), extent[axis_at] // parts).reshape((-1,) + (1,) * (len(extent) - axis_at - 1))

    factor_of = one(*shards[0])
    for cut in shards[1:]:
        factor_of = factor_of * one(*cut)
    return factor_of


def centred(own_key, shape, deviation, most, cuts=(), held_as=jnp.bfloat16):
    gain = levels(own_key, shape, cuts, -0.22, 0.18) if cuts else 1.0
    drawn = jax.random.normal(own_key, shape, jnp.float32) * deviation * gain
    return jnp.minimum(jnp.maximum(drawn, -most), most).astype(held_as)


def setup_inputs(seed: int = 0) -> dict:
    streams_of = jax.random.split(jax.random.key(seed), 7)
    return {
        "points": centred(streams_of[0], (DIM, POINTS), 1.0, 6.0, ((1, 128),)),
        "weights": centred(streams_of[1], (POINTS, RHS), 0.2, 1.1953125, ((0, 128),)),
        "interp": centred(streams_of[2], (POINTS, S), NPTS ** -0.5, 0.1875, ((0, 128),)),
        "transfers": centred(streams_of[3], (LEAVES, LEVELS, S, S), S ** -0.5, 0.25, ((0, 128),)),
        "near_mask": set_ends((jax.random.randint(streams_of[4], (LEAVES, 2 * RADIUS), 0, 4) < 3).astype(jnp.int32), jax.random.fold_in(streams_of[4], 1), 0, 1),
        "skel_index": draw_skel_index(jax.random.fold_in(streams_of[6], 71), 0),
    }


def widened(value):
    return lax.optimization_barrier(value).astype(jnp.float32)


def kernel_tile(left, right):
    left_wide = left.astype(jnp.float32)
    right_wide = right.astype(jnp.float32)
    sq_left = jnp.sum(left_wide * left_wide, axis=0)
    sq_right = jnp.sum(right_wide * right_wide, axis=0)
    cross_terms = lax.dot_general(left, right, (((0,), (0,)), ((), ())), preferred_element_type=jnp.float32)
    distance = sq_left[:, None] + sq_right[None, :] - 2.0 * cross_terms
    return jnp.exp(distance * (-1.0 / DIM)).astype(jnp.bfloat16)


def reference(points, weights, interp, transfers, near_mask, skel_index):
    leaf_points = points.reshape(DIM, LEAVES, NPTS).transpose(1, 0, 2)
    leaf_weights_in = weights.reshape(LEAVES, NPTS, RHS)
    leaf_interp = interp.reshape(LEAVES, NPTS, S)
    offsets = list(range(-RADIUS, 0)) + list(range(1, RADIUS + 1))

    def near_leaf(leaf_id):
        own_points = leaf_points[leaf_id]
        total = jnp.dot(kernel_tile(own_points, own_points), leaf_weights_in[leaf_id], preferred_element_type=jnp.float32)
        for slot_index, offset in enumerate(offsets):
            target = leaf_id + offset
            neighbour = jnp.clip(target, 0, LEAVES - 1)
            in_range = (target >= 0) & (target < LEAVES)
            flag_value = jnp.where(in_range, near_mask[leaf_id, slot_index], 0).astype(jnp.float32)
            block = jnp.dot(kernel_tile(own_points, leaf_points[neighbour]), leaf_weights_in[neighbour], preferred_element_type=jnp.float32)
            total = total + flag_value * block
        return total

    leaf_ids = jnp.arange(LEAVES, dtype=jnp.int32)
    near_field = lax.map(near_leaf, leaf_ids)
    skel_points = jnp.take_along_axis(leaf_points, skel_index[:, None, :], axis=2)
    leaf_weights = jnp.einsum("nps,npr->nsr", widened(leaf_interp), widened(leaf_weights_in)).astype(jnp.bfloat16)
    far_sum = jnp.zeros((LEAVES, S, RHS), jnp.float32)
    for level in range(LEVELS):
        transfer_level = widened(transfers[:, level])
        level_terms = jnp.einsum("nab,nar->nbr", transfer_level, widened(leaf_weights))
        nodes = LEAVES >> level
        group = 2 ** level
        node_sums = level_terms.reshape(nodes, group, S, RHS).sum(axis=1).astype(jnp.bfloat16)
        columns_kept = S >> level
        node_points = skel_points[:, :, :columns_kept].reshape(nodes, group, DIM, columns_kept)
        node_points = node_points.transpose(0, 2, 1, 3).reshape(nodes, DIM, S)

        def couple_node(node_id):
            partner = node_id ^ 1
            tile = kernel_tile(node_points[node_id], node_points[partner])
            return jnp.dot(tile, node_sums[partner], preferred_element_type=jnp.float32).astype(jnp.bfloat16)

        coupled = lax.map(couple_node, jnp.arange(nodes, dtype=jnp.int32))
        coupled_leaf = jnp.repeat(coupled, group, axis=0)
        far_sum = far_sum + jnp.einsum("nab,nbr->nar", transfer_level, widened(coupled_leaf))
    far_skeleton = far_sum.astype(jnp.bfloat16)
    far_field = jnp.einsum("nps,nsr->npr", widened(leaf_interp), widened(far_skeleton))
    return (near_field + far_field).astype(jnp.bfloat16).reshape(POINTS, RHS)
```

```python
import math

import jax
import jax.numpy as jnp
from jax import lax
from jax.experimental import pallas as pl
from jax.experimental.pallas import tpu as pltpu
from jax.sharding import PartitionSpec as P

F32 = jnp.float32
BF16 = jnp.bfloat16
AXIS = "leaf"
VMEM_BYTES = 48 * 1024 * 1024
ROWS = 256


def dot(a, b, over=((1,), (0,))):
    return lax.dot_general(a, b, (over, ((), ())), preferred_element_type=F32)


def place():
    leaf = lax.axis_index(AXIS)
    return leaf & 1, (leaf >> 1) & 3, (leaf >> 3) & 3


def split_norm(wide, scale):
    norm = jnp.sum(wide * wide, axis=0, keepdims=True) * scale
    high = norm.astype(BF16).astype(F32)
    rest = norm - high
    middle = rest.astype(BF16).astype(F32)
    return high, middle, rest - middle


def lifted(points, left):
    dim, count = points.shape
    scale = math.log2(math.e) / dim
    wide = points.astype(F32)
    high, middle, low = split_norm(wide, -scale)
    row = lax.broadcasted_iota(jnp.int32, (16, count), 0)
    at = 0 if left else 3
    ones = 3 - at
    extra = jnp.where(row == at, high, jnp.where(row == at + 1, middle, jnp.where(row == at + 2, low, 0.0)))
    extra = jnp.where((row >= ones) & (row < ones + 3), 1.0, extra).astype(BF16)
    if left:
        scaled = wide * (2.0 * scale)
        first = scaled.astype(BF16)
        second = (scaled - first.astype(F32)).astype(BF16)
    else:
        first = second = points
    return jnp.concatenate([first, second, extra], axis=0)


def gaussian(left, right):
    return jnp.exp2(dot(left, right, ((0,), (0,)))).astype(BF16)


def call(body, name, outs, args, flops, smem=(), scratch=(), grid=None, in_specs=None):
    specs = in_specs or [pl.BlockSpec(memory_space=pltpu.SMEM if k in smem else pltpu.VMEM) for k in range(len(args))]
    moved = sum(a.size * a.dtype.itemsize for a in args) + sum(math.prod(s) * jnp.dtype(t).itemsize for s, t in outs)
    return pl.pallas_call(
        body,
        name=name,
        grid=grid or (),
        in_specs=specs,
        out_specs=[pl.BlockSpec(memory_space=pltpu.VMEM) for _ in outs],
        out_shape=[jax.ShapeDtypeStruct(s, t) for s, t in outs],
        scratch_shapes=list(scratch),
        compiler_params=pltpu.CompilerParams(vmem_limit_bytes=VMEM_BYTES),
        cost_estimate=pl.CostEstimate(flops=int(flops), bytes_accessed=int(moved), transcendentals=0),
    )(*args)


def pack(half):
    return jnp.concatenate([half[:32], half[32:]], axis=1)


def unpack(packed):
    return jnp.concatenate([packed[:, :256], packed[:, 256:]], axis=0)


def picked(columns, count, wide, kept):
    source = lax.broadcasted_iota(jnp.int32, (columns.shape[1], count), 0)
    target = lax.broadcasted_iota(jnp.int32, (columns.shape[1], count), 1)
    choice = (source == (target // kept) * wide + target % kept).astype(F32).astype(BF16)
    return dot(columns, choice).astype(BF16)


def terms_kernel(w, p, t, pts, index, term0, send, keep, skel, lifted_weights):
    step = pl.program_id(0)
    core, _, _ = place()

    @pl.when(step == 0)
    def _():
        lifted_weights[...] = dot(w[...], p[...], ((0,), (0,))).astype(BF16)
        rank = lax.broadcasted_iota(jnp.int32, (pts.shape[1], index.shape[1]), 0)
        choice = (rank == index[...]).astype(F32).astype(BF16)
        chosen = dot(pts[...], choice).astype(BF16)
        skel[...] = chosen
        send[1024:1088, :] = chosen

    @pl.when(step < 4)
    def _():
        row = pl.multiple_of(step * 256, 256)
        theirs = pl.multiple_of((1 - core) * 256, 256)
        mine = pl.multiple_of(core * 256, 256)
        send[pl.ds(row, 256), :] = dot(lifted_weights[pl.ds(theirs, 256), :], t[0, 0]).astype(BF16)
        keep[pl.ds(row, 256), :] = dot(lifted_weights[pl.ds(mine, 256), :], t[0, 0])

    @pl.when(step == 4)
    def _():
        term0[...] = dot(lifted_weights[...], t[0, 0]).astype(BF16)


def chip_kernel(keep, came, skel, to2, to4, to6, kept, pair, total):
    core, x, _ = place()
    mine, theirs = skel[...], came[1024:1088, :]
    first = jnp.where(core == 0, mine, theirs)
    second = jnp.where(core == 0, theirs, mine)
    pair[0:64, :] = first
    pair[64:128, :] = second
    total[...] = keep[...] + came[0:1024, :].astype(F32)
    to2[0:256, :] = total[0:256, :].astype(BF16)
    to2[384:448, :] = jnp.concatenate([first[:, :256], second[:, :256]], axis=1)
    for level, at in ((3, 0), (4, 64)):
        for out, row, other in ((to2, 256, x ^ 1), (to4, 128, x ^ 2), (to6, 128, x ^ 3)):
            rows = pl.ds(pl.multiple_of((level - 1) * 256 + other * 64, 64), 64)
            out[row + at : row + at + 64, :] = total[rows, :].astype(BF16)
        kept[at : at + 64, :] = total[pl.ds(pl.multiple_of((level - 1) * 256 + x * 64, 64), 64), :]
    packed = pack(jnp.concatenate([first[:, :128], second[:, :128]], axis=1))
    for out, part in ((to4, x & 1), (to6, (x & 1) ^ 1)):
        out[0:128, :] = total[pl.ds(pl.multiple_of(256 + part * 128, 128), 128), :].astype(BF16)
        out[256:288, :] = packed


def row_kernel(from2, from4, from6, kept, pair, to8, to16, ring):
    _, x, _ = place()
    near = from2[384:448, :]
    ring[x] = jnp.concatenate([pair[0:64, 0:128], pair[64:128, 0:128]], axis=1)
    ring[x ^ 1] = jnp.concatenate([near[:, 0:128], near[:, 256:384]], axis=1)
    ring[x ^ 2] = unpack(from4[256:288, :])
    ring[x ^ 3] = unpack(from6[256:288, :])
    points3 = picked(jnp.concatenate([ring[k] for k in range(4)], axis=1), 512, 128, 64)
    for out, at in ((to8, 0), (to16, 64)):
        total = kept[at : at + 64, :] + from2[256 + at : 320 + at, :].astype(F32)
        total = total + from4[128 + at : 192 + at, :].astype(F32) + from6[128 + at : 192 + at, :].astype(F32)
        out[0:64, :] = total.astype(BF16)
    to8[64:128, :] = points3
    to16[64:96, :] = pack(picked(points3, 256, 64, 32))


def couple(sums, own, sibling):
    return dot(sums, gaussian(lifted(sibling, True), lifted(own, False))).astype(BF16)


def couple_low_kernel(term0, from2, from4, from6, pair, ring, out0, out1, out2):
    core, x, _ = place()
    first, second = pair[0:64, :], pair[64:128, :]
    out0[...] = couple(term0[...], jnp.where(core == 0, first, second), jnp.where(core == 0, second, first))
    own = jnp.concatenate([first[:, :256], second[:, :256]], axis=1)
    out1[...] = couple(from2[0:256, :], own, from2[384:448, :])
    low = x & 2
    own = jnp.concatenate([ring[low], ring[low | 1]], axis=1)
    sibling = jnp.concatenate([ring[low ^ 2], ring[(low ^ 2) | 1]], axis=1)
    sums = (from4[0:128, :].astype(F32) + from6[0:128, :].astype(F32)).astype(BF16)
    out2[...] = couple(sums, own, sibling)


def couple_high_kernel(from8, from16, from24, to8, to16, coupled2, out2, out4):
    _, _, z = place()
    points3 = from8[64:128, :]
    level3 = couple(from8[0:64, :], to8[64:128, :], points3)
    mine, beside = unpack(to16[64:96, :]), picked(points3, 256, 64, 32)
    even = (z & 1) == 0
    own = jnp.concatenate([jnp.where(even, mine, beside), jnp.where(even, beside, mine)], axis=1)
    across, past = unpack(from16[64:96, :]), unpack(from24[64:96, :])
    sibling = jnp.concatenate([jnp.where(even, across, past), jnp.where(even, past, across)], axis=1)
    sums = (from16[0:64, :].astype(F32) + from24[0:64, :].astype(F32)).astype(BF16)
    level4 = couple(sums, own, sibling)
    out2[0:64, :] = level3
    out2[64:128, :] = level4
    out2[128:256, :] = coupled2[...]
    out4[0:64, :] = level3
    out4[64:128, :] = level4


def half_kernel(coupled1, own, from2, from4, from6, out):
    _, x, _ = place()
    out[0:256, :] = coupled1[...]
    out[pl.ds(pl.multiple_of(256 + (x & 1) * 128, 128), 128), :] = own[128:256, :]
    out[pl.ds(pl.multiple_of(256 + ((x & 1) ^ 1) * 128, 128), 128), :] = from2[128:256, :]
    for base, at in ((512, 0), (768, 64)):
        for part, block in ((x, own), (x ^ 1, from2), (x ^ 2, from4), (x ^ 3, from6)):
            out[pl.ds(pl.multiple_of(base + part * 64, 64), 64), :] = block[at : at + 64, :]


def near_kernel(count, slots, with_total, *refs):
    mask, own = refs[0], refs[1]
    blocks = refs[2 : 2 + count]
    total = refs[2 + count] if with_total else None
    out = refs[-1]
    core, _, _ = place()
    size = own.shape[1]
    left = lifted(own[...], True)
    result = [None] * (size // ROWS)
    for block, slot in zip(blocks, slots):
        if slot is None:
            right = lifted(own[...], False)
        else:
            columns = jnp.concatenate([block[size : size + 64, :], block[size + 64 : size + 128, :]], axis=1)
            right = lifted(columns, False)
            flag = jnp.where(core == 0, mask[0, slot[0]], mask[0, slot[1]]).astype(F32)
        values = block[0:size, :]
        for k in range(size // ROWS):
            tile = gaussian(left[:, k * ROWS : (k + 1) * ROWS], right)
            part = dot(tile, values)
            if slot is not None:
                part = part * flag
            result[k] = part if result[k] is None else result[k] + part
    for k in range(size // ROWS):
        rows = slice(k * ROWS, (k + 1) * ROWS)
        out[rows, :] = result[k] + total[rows, :] if with_total else result[k]


def near(mask, points, blocks, slots, total, name):
    args = [mask, points, *blocks] + ([] if total is None else [total])
    size, width = points.shape[1], blocks[0].shape[1]

    def body(*refs):
        near_kernel(len(blocks), slots, total is not None, *refs)

    flops = 2 * len(blocks) * size * size * (width + 256)
    return call(body, name, [((size, width), F32)], args, flops, smem=(0,))[0]


def product_kernel(total, interp, transfers, coupled0, mine, theirs, out, far):
    core, _, _ = place()
    base = dot(transfers[0, 0], coupled0[...], ((1,), (1,)))
    far[...] = base
    for part, half in ((core, mine), (1 - core, theirs)):
        columns = pl.ds(pl.multiple_of(part * 256, 256), 256)
        value = far[:, columns]
        for level in range(1, 5):
            value = value + dot(transfers[0, level], half[(level - 1) * 256 : level * 256, :], ((1,), (1,)))
        far[:, columns] = value
    skeleton = far[...].astype(BF16)
    for k in range(total.shape[0] // ROWS):
        rows = slice(k * ROWS, (k + 1) * ROWS)
        out[rows, :] = (total[rows, :] + dot(interp[rows, :], skeleton)).astype(BF16)


def per_device(points, weights, interp, transfers, near_mask, skel_index):
    leaves = lax.axis_size(AXIS)
    size, width = weights.shape

    def swap(value, mask):
        return lax.ppermute(value, AXIS, [(leaf, leaf ^ mask) for leaf in range(leaves)])

    def moved(value, even, odd):
        pairs = [(leaf, leaf + (odd if leaf & 1 else even)) for leaf in range(leaves)]
        return lax.ppermute(value, AXIS, [(a, b) for a, b in pairs if 0 <= b < leaves])

    payload = jnp.concatenate([weights, points[:, : size // 2], points[:, size // 2 :]], axis=0)
    outer = moved(payload, -1, 1)
    partner = swap(payload, 1)

    whole = lambda *shape: pl.BlockSpec(shape, lambda g: (0,) * len(shape))
    term0, send, keep, skel = call(
        terms_kernel,
        "terms",
        [((512, 512), BF16), ((1088, 512), BF16), ((1024, 512), F32), ((64, 512), BF16)],
        [weights, interp, transfers, points, skel_index],
        2 * 512 * 512 * (1024 + 5 * 512),
        scratch=[pltpu.VMEM((512, 512), BF16)],
        grid=(5,),
        in_specs=[
            whole(size, width),
            whole(size, 512),
            pl.BlockSpec((1, 1, 512, 512), lambda g: (0, lax.rem(g + 1, 5), 0, 0)),
            whole(64, size),
            whole(1, 512),
        ],
    )
    came = swap(send, 1)
    term0 = swap(term0, 1)
    total = near(near_mask, points, [weights, partner], [None, (2, 1)], None, "near_own")

    to2, to4, to6, kept, pair = call(
        chip_kernel,
        "chip",
        [((448, 512), BF16), ((288, 512), BF16), ((288, 512), BF16), ((128, 512), F32), ((128, 512), BF16)],
        [keep, came, skel],
        1e6,
        scratch=[pltpu.VMEM((1024, 512), F32)],
    )
    from2, from4, from6 = swap(to2, 2), swap(to4, 4), swap(to6, 6)
    past = swap(outer, 1)
    second = moved(payload, 2, -2)

    to8, to16, ring = call(
        row_kernel,
        "row",
        [((128, 512), BF16), ((96, 512), BF16), ((4, 64, 256), BF16)],
        [from2, from4, from6, kept, pair],
        1e8,
    )
    from8, from16, from24 = swap(to8, 8), swap(to16, 16), swap(to16, 24)
    coupled0, coupled1, coupled2 = call(
        couple_low_kernel,
        "couple_low",
        [((512, 512), BF16), ((256, 512), BF16), ((128, 512), BF16)],
        [term0, from2, from4, from6, pair, ring],
        2 * 512 * 512 * (3 * 256 + 896),
    )
    total = near(near_mask, points, [outer, past], [(1, 2), (3, 0)], total, "near_outer")
    part2, part4 = call(
        couple_high_kernel,
        "couple_high",
        [((256, 512), BF16), ((128, 512), BF16)],
        [from8, from16, from24, to8, to16, coupled2],
        2 * 512 * 512 * (2 * 256 + 128),
    )
    back2, back4, back6 = swap(part2, 2), swap(part4, 4), swap(part4, 6)
    (mine,) = call(half_kernel, "half", [((1024, 512), BF16)], [coupled1, part2, back2, back4, back6], 1e6)
    theirs = swap(mine, 1)
    total = near(near_mask, points, [second], [(0, 3)], total, "near_second")
    return call(
        product_kernel,
        "product",
        [((size, width), BF16)],
        [total, interp, transfers, coupled0, mine, theirs],
        2 * 512 * 512 * (5 * 512 + 1024),
        scratch=[pltpu.VMEM((512, 512), F32)],
    )[0]


def solution(mesh):
    return jax.shard_map(
        per_device,
        mesh=mesh,
        in_specs=(
            P(None, AXIS),
            P(AXIS, None),
            P(AXIS, None),
            P(AXIS, None, None, None),
            P(AXIS, None),
            P(AXIS, None),
        ),
        out_specs=P(AXIS, None),
        check_vma=False,
    )
```

```python
import math

import jax
import jax.numpy as jnp
from jax import lax
from jax.experimental import pallas as pl
from jax.experimental.pallas import tpu as pltpu
from jax.sharding import PartitionSpec as P

F32 = jnp.float32
BF16 = jnp.bfloat16
AXIS = "leaf"
VMEM_BYTES = 24 * 1024 * 1024
ROWS = 256
WORK = 1.0


def dot(a, b, over=((1,), (0,))):
    return lax.dot_general(a, b, (over, ((), ())), preferred_element_type=F32)


def place():
    leaf = lax.axis_index(AXIS)
    return leaf & 1, (leaf >> 1) & 3, (leaf >> 3) & 3


def split_norm(wide, scale):
    norm = jnp.sum(wide * wide, axis=0, keepdims=True) * scale
    high = norm.astype(BF16).astype(F32)
    rest = norm - high
    middle = rest.astype(BF16).astype(F32)
    return high, middle, rest - middle


def lifted(points, left):
    dim, count = points.shape
    scale = math.log2(math.e) / dim
    wide = points.astype(F32)
    high, middle, low = split_norm(wide, -scale)
    row = lax.broadcasted_iota(jnp.int32, (16, count), 0)
    at = 0 if left else 3
    ones = 3 - at
    extra = jnp.where(row == at, high, jnp.where(row == at + 1, middle, jnp.where(row == at + 2, low, 0.0)))
    extra = jnp.where((row >= ones) & (row < ones + 3), 1.0, extra).astype(BF16)
    if left:
        scaled = wide * (2.0 * scale)
        first = scaled.astype(BF16)
        second = (scaled - first.astype(F32)).astype(BF16)
    else:
        first = second = points
    return jnp.concatenate([first, second, extra], axis=0)


def gaussian(left, right):
    return jnp.exp2(dot(left, right, ((0,), (0,)))).astype(BF16)


def call(body, name, outs, args, flops, smem=(), scratch=(), grid=None, in_specs=None, after=()):
    specs = in_specs or [pl.BlockSpec(memory_space=pltpu.SMEM if k in smem else pltpu.VMEM) for k in range(len(args))]
    specs = specs + [pl.BlockSpec(memory_space=pl.ANY) for _ in after]
    taken = len(args)

    def reading(*refs):
        body(*refs[:taken], *refs[taken + len(after) :])

    moved = sum(a.size * a.dtype.itemsize for a in args) + sum(math.prod(s) * jnp.dtype(t).itemsize for s, t in outs)
    return pl.pallas_call(
        reading,
        name=name,
        grid=grid or (),
        in_specs=specs,
        out_specs=[pl.BlockSpec(memory_space=pltpu.VMEM) for _ in outs],
        out_shape=[jax.ShapeDtypeStruct(s, t) for s, t in outs],
        scratch_shapes=list(scratch),
        compiler_params=pltpu.CompilerParams(vmem_limit_bytes=VMEM_BYTES),
        cost_estimate=pl.CostEstimate(flops=int(flops * WORK), bytes_accessed=int(moved * WORK), transcendentals=0),
    )(*args, *after)


def pack(half):
    return jnp.concatenate([half[:32], half[32:]], axis=1)


def unpack(packed):
    return jnp.concatenate([packed[:, :256], packed[:, 256:]], axis=0)


def picked(columns, count, wide, kept):
    source = lax.broadcasted_iota(jnp.int32, (columns.shape[1], count), 0)
    target = lax.broadcasted_iota(jnp.int32, (columns.shape[1], count), 1)
    choice = (source == (target // kept) * wide + target % kept).astype(F32).astype(BF16)
    return dot(columns, choice).astype(BF16)


def pack_kernel(points, weights, out, done):
    half = points.shape[1] // 2
    rows = weights.shape[0]
    copies = [
        pltpu.make_async_copy(weights, out.at[0:rows, :], done.at[0]),
        pltpu.make_async_copy(points.at[:, 0:half], out.at[rows : rows + 64, :], done.at[1]),
        pltpu.make_async_copy(points.at[:, half : 2 * half], out.at[rows + 64 : rows + 128, :], done.at[2]),
    ]
    for copy in copies:
        copy.start()
    for copy in copies:
        copy.wait()


def terms_kernel(w, p, t, send, keep, lifted_weights):
    step = pl.program_id(0)
    core, _, _ = place()

    @pl.when(step == 0)
    def _():
        lifted_weights[...] = dot(w[0:1024, :], p[...], ((0,), (0,))).astype(BF16)

    row = pl.multiple_of(step * 256, 256)
    theirs = pl.multiple_of((1 - core) * 256, 256)
    mine = pl.multiple_of(core * 256, 256)
    send[pl.ds(row, 256), :] = dot(lifted_weights[pl.ds(theirs, 256), :], t[0, 0]).astype(BF16)
    keep[pl.ds(row, 256), :] = dot(lifted_weights[pl.ds(mine, 256), :], t[0, 0])


def leaf_kernel(lifted_weights, t, payload, index, out):
    size = payload.shape[0] - 128
    out[0:512, :] = dot(lifted_weights[...], t[0, 0]).astype(BF16)
    rank = lax.broadcasted_iota(jnp.int32, (size // 2, index.shape[1]), 0)
    chosen = dot(payload[size : size + 64, :], (rank == index[...]).astype(F32).astype(BF16))
    chosen = chosen + dot(payload[size + 64 : size + 128, :], (rank + size // 2 == index[...]).astype(F32).astype(BF16))
    out[512:576, :] = chosen.astype(BF16)


def chip_kernel(keep, came, mine, theirs, to1, to2, to4, to6, kept, pair, total):
    core, x, _ = place()
    mine, theirs = mine[512:576, :], theirs[512:576, :]
    first = jnp.where(core == 0, mine, theirs)
    second = jnp.where(core == 0, theirs, mine)
    pair[0:64, :] = first
    pair[64:128, :] = second
    total[...] = keep[...] + came[...].astype(F32)
    to1[...] = total[0:256, :].astype(BF16)
    to2[128:192, :] = jnp.concatenate([first[:, :256], second[:, :256]], axis=1)
    for level, at in ((3, 0), (4, 64)):
        for out, row, other in ((to2, 0, x ^ 1), (to4, 128, x ^ 2), (to6, 128, x ^ 3)):
            rows = pl.ds(pl.multiple_of((level - 1) * 256 + other * 64, 64), 64)
            out[row + at : row + at + 64, :] = total[rows, :].astype(BF16)
        kept[at : at + 64, :] = total[pl.ds(pl.multiple_of((level - 1) * 256 + x * 64, 64), 64), :]
    packed = pack(jnp.concatenate([first[:, :128], second[:, :128]], axis=1))
    for out, part in ((to4, x & 1), (to6, (x & 1) ^ 1)):
        out[0:128, :] = total[pl.ds(pl.multiple_of(256 + part * 128, 128), 128), :].astype(BF16)
        out[256:288, :] = packed


def row_kernel(from2, from4, from6, kept, pair, to8, to16, ring):
    _, x, _ = place()
    near = from2[128:192, :]
    ring[x] = jnp.concatenate([pair[0:64, 0:128], pair[64:128, 0:128]], axis=1)
    ring[x ^ 1] = jnp.concatenate([near[:, 0:128], near[:, 256:384]], axis=1)
    ring[x ^ 2] = unpack(from4[256:288, :])
    ring[x ^ 3] = unpack(from6[256:288, :])
    points3 = picked(jnp.concatenate([ring[k] for k in range(4)], axis=1), 512, 128, 64)
    for out, at in ((to8, 0), (to16, 64)):
        total = kept[at : at + 64, :] + from2[at : 64 + at, :].astype(F32)
        total = total + from4[128 + at : 192 + at, :].astype(F32) + from6[128 + at : 192 + at, :].astype(F32)
        out[0:64, :] = total.astype(BF16)
    to8[64:128, :] = points3
    to16[64:96, :] = pack(picked(points3, 256, 64, 32))


def couple(sums, own, sibling):
    return dot(sums, gaussian(lifted(sibling, True), lifted(own, False))).astype(BF16)


def couple_low_kernel(term0, from4, from6, pair, ring, out0, out2):
    core, x, _ = place()
    first, second = pair[0:64, :], pair[64:128, :]
    out0[...] = couple(term0[0:512, :], jnp.where(core == 0, first, second), jnp.where(core == 0, second, first))
    low = x & 2
    own = jnp.concatenate([ring[low], ring[low | 1]], axis=1)
    sibling = jnp.concatenate([ring[low ^ 2], ring[(low ^ 2) | 1]], axis=1)
    sums = (from4[0:128, :].astype(F32) + from6[0:128, :].astype(F32)).astype(BF16)
    out2[...] = couple(sums, own, sibling)


def couple_chip_kernel(sums, from2, pair, out1):
    own = jnp.concatenate([pair[0:64, 0:256], pair[64:128, 0:256]], axis=1)
    out1[...] = couple(sums[...], own, from2[128:192, :])


def couple_high_kernel(from8, from16, from24, to8, to16, coupled2, out2, out4):
    _, _, z = place()
    points3 = from8[64:128, :]
    level3 = couple(from8[0:64, :], to8[64:128, :], points3)
    mine, beside = unpack(to16[64:96, :]), picked(points3, 256, 64, 32)
    even = (z & 1) == 0
    own = jnp.concatenate([jnp.where(even, mine, beside), jnp.where(even, beside, mine)], axis=1)
    across, past = unpack(from16[64:96, :]), unpack(from24[64:96, :])
    sibling = jnp.concatenate([jnp.where(even, across, past), jnp.where(even, past, across)], axis=1)
    sums = (from16[0:64, :].astype(F32) + from24[0:64, :].astype(F32)).astype(BF16)
    level4 = couple(sums, own, sibling)
    out2[0:64, :] = level3
    out2[64:128, :] = level4
    out2[128:256, :] = coupled2[...]
    out4[0:64, :] = level3
    out4[64:128, :] = level4


def half_kernel(coupled1, own, from2, from4, from6, out):
    _, x, _ = place()
    out[0:256, :] = coupled1[...]
    out[pl.ds(pl.multiple_of(256 + (x & 1) * 128, 128), 128), :] = own[128:256, :]
    out[pl.ds(pl.multiple_of(256 + ((x & 1) ^ 1) * 128, 128), 128), :] = from2[128:256, :]
    for base, at in ((512, 0), (768, 64)):
        for part, block in ((x, own), (x ^ 1, from2), (x ^ 2, from4), (x ^ 3, from6)):
            out[pl.ds(pl.multiple_of(base + part * 64, 64), 64), :] = block[at : at + 64, :]


def near_kernel(count, slots, with_total, *refs):
    mask, own = refs[0], refs[1]
    blocks = refs[2 : 2 + count]
    total = refs[2 + count] if with_total else None
    out, token = refs[-2], refs[-1]
    token[...] = jnp.zeros_like(token)
    core, _, _ = place()
    size = own.shape[1]
    left = lifted(own[...], True)
    result = [None] * (size // ROWS)
    for block, slot in zip(blocks, slots):
        if slot is None:
            right = lifted(own[...], False)
        else:
            columns = jnp.concatenate([block[size : size + 64, :], block[size + 64 : size + 128, :]], axis=1)
            right = lifted(columns, False)
            flag = jnp.where(core == 0, mask[0, slot[0]], mask[0, slot[1]]).astype(F32)
        values = block[0:size, :]
        for k in range(size // ROWS):
            tile = gaussian(left[:, k * ROWS : (k + 1) * ROWS], right)
            part = dot(tile, values)
            if slot is not None:
                part = part * flag
            result[k] = part if result[k] is None else result[k] + part
    for k in range(size // ROWS):
        rows = slice(k * ROWS, (k + 1) * ROWS)
        out[rows, :] = result[k] + total[rows, :] if with_total else result[k]


def near(mask, points, blocks, slots, total, name, after):
    args = [mask, points, *blocks] + ([] if total is None else [total])
    size, width = points.shape[1], blocks[0].shape[1]

    def body(*refs):
        near_kernel(len(blocks), slots, total is not None, *refs)

    flops = 2 * len(blocks) * size * size * (width + 256)
    return call(body, name, [((size, width), F32), ((8, 128), F32)], args, flops, smem=(0,), after=after)


def add_levels(far, transfers, half, part):
    columns = pl.ds(pl.multiple_of(part * 256, 256), 256)
    value = far[:, columns]
    for level in range(1, 5):
        value = value + dot(transfers[0, level], half[(level - 1) * 256 : level * 256, :], ((1,), (1,)))
    far[:, columns] = value


def far_kernel(transfers, coupled0, mine, far):
    core, _, _ = place()
    far[...] = dot(transfers[0, 0], coupled0[...], ((1,), (1,)))
    add_levels(far, transfers, mine, core)


def product_kernel(total, interp, transfers, begun, theirs, out, far):
    core, _, _ = place()
    far[...] = begun[...]
    add_levels(far, transfers, theirs, 1 - core)
    skeleton = far[...].astype(BF16)
    for k in range(total.shape[0] // ROWS):
        rows = slice(k * ROWS, (k + 1) * ROWS)
        out[rows, :] = (total[rows, :] + dot(interp[rows, :], skeleton)).astype(BF16)


def per_device(points, weights, interp, transfers, near_mask, skel_index):
    leaves = lax.axis_size(AXIS)
    size, width = weights.shape

    def swap(value, mask):
        return lax.ppermute(value, AXIS, [(leaf, leaf ^ mask) for leaf in range(leaves)])

    def moved(value, even, odd):
        pairs = [(leaf, leaf + (odd if leaf & 1 else even)) for leaf in range(leaves)]
        return lax.ppermute(value, AXIS, [(a, b) for a, b in pairs if 0 <= b < leaves])

    def rows(count, dtype=BF16):
        return (count, 512), dtype

    def whole(*shape):
        return pl.BlockSpec(shape, lambda g: (0,) * len(shape))

    def near_of(blocks, slots, total, name, after):
        return near(near_mask, points, blocks, slots, total, name, after)

    (payload,) = call(
        pack_kernel,
        "pack",
        [rows(size + 128)],
        [points, weights],
        0,
        scratch=[pltpu.SemaphoreType.DMA((3,))],
        in_specs=[pl.BlockSpec(memory_space=pl.ANY)] * 2,
    )
    outer = moved(payload, -1, 1)
    second = moved(payload, 2, -2)
    partner = swap(payload, 1)
    send, keep, lifted_weights = call(
        terms_kernel,
        "terms",
        [rows(1024), rows(1024, F32), rows(512)],
        [payload, interp, transfers],
        2 * 512 * 512 * (1024 + 4 * 512),
        grid=(4,),
        in_specs=[
            whole(size + 128, width),
            whole(size, 512),
            pl.BlockSpec((1, 1, 512, 512), lambda g: (0, g + 1, 0, 0)),
        ],
    )
    came = swap(send, 1)
    (term0,) = call(
        leaf_kernel,
        "leaf",
        [rows(576)],
        [lifted_weights, transfers, payload, skel_index],
        2 * 512 * 512 * 768,
        grid=(1,),
        in_specs=[
            whole(512, 512),
            pl.BlockSpec((1, 1, 512, 512), lambda g: (0, 0, 0, 0)),
            whole(size + 128, width),
            whole(1, 512),
        ],
    )
    other0 = swap(term0, 1)
    total, token = near_of([payload, partner], [None, (2, 1)], None, "near_own", (term0,))

    to1, to2, to4, to6, kept, pair = call(
        chip_kernel,
        "chip",
        [rows(256), rows(192), rows(288), rows(288), rows(128, F32), rows(128)],
        [keep, came, term0, other0],
        1e6,
        after=(token,),
        scratch=[pltpu.VMEM((1024, 512), F32)],
    )
    from2, from4, from6 = swap(to2, 2), swap(to4, 4), swap(to6, 6)
    total, token = near_of([outer], [(1, 2)], total, "near_outer", (pair,))

    total, token = near_of([second], [(0, 3)], total, "near_second", (token,))
    to8, to16, ring = call(
        row_kernel,
        "row",
        [rows(128), rows(96), ((4, 64, 256), BF16)],
        [from2, from4, from6, kept, pair],
        1e8,
        after=(token,),
    )
    from8, from16, from24 = swap(to8, 8), swap(to16, 16), swap(to16, 24)
    to1, outer, ring = lax.optimization_barrier((to1, outer, ring))
    from1 = swap(to1, 2)
    past = swap(outer, 1)
    coupled0, coupled2 = call(
        couple_low_kernel,
        "couple_low",
        [rows(512), rows(128)],
        [other0, from4, from6, pair, ring],
        40 * 512 * 512 * (2 * 256 + 640),
    )
    part2, part4 = call(
        couple_high_kernel,
        "couple_high",
        [rows(256), rows(128)],
        [from8, from16, from24, to8, to16, coupled2],
        2 * 512 * 512 * (2 * 256 + 128),
    )
    back2, back4, back6 = swap(part2, 2), swap(part4, 4), swap(part4, 6)
    (coupled1,) = call(
        couple_chip_kernel, "couple_chip", [rows(256)], [from1, from2, pair], 2 * 512 * 512 * 512, after=(part4,)
    )
    total, token = near_of([past], [(3, 0)], total, "near_past", (coupled1,))
    (mine,) = call(
        half_kernel, "half", [rows(1024)], [coupled1, part2, back2, back4, back6], 1e6, after=(token,)
    )
    theirs = swap(mine, 1)
    (far,) = call(far_kernel, "far", [rows(512, F32)], [transfers, coupled0, mine], 2 * 512 * 512 * 5 * 400)
    return call(
        product_kernel,
        "product",
        [((size, width), BF16)],
        [total, interp, transfers, far, theirs],
        2 * 512 * 512 * (4 * 256 + 1024),
        scratch=[pltpu.VMEM((512, 512), F32)],
    )[0]


def solution(mesh):
    return jax.shard_map(
        per_device,
        mesh=mesh,
        in_specs=(
            P(None, AXIS),
            P(AXIS, None),
            P(AXIS, None),
            P(AXIS, None, None, None),
            P(AXIS, None),
            P(AXIS, None),
        ),
        out_specs=P(AXIS, None),
        check_vma=False,
    )
```

```python
import math

import jax
import jax.numpy as jnp
from jax import lax
from jax.experimental import pallas as pl
from jax.experimental.pallas import tpu as pltpu
from jax.sharding import PartitionSpec as P

F32 = jnp.float32
BF16 = jnp.bfloat16
AXIS = "leaf"
VMEM_BYTES = 24 * 1024 * 1024
ROWS = 256
WORK = 1.0
LOW = 1.0


def dot(a, b, over=((1,), (0,))):
    return lax.dot_general(a, b, (over, ((), ())), preferred_element_type=F32)


def place():
    leaf = lax.axis_index(AXIS)
    return leaf & 1, (leaf >> 1) & 3, (leaf >> 3) & 3


def split_norm(wide, scale):
    norm = jnp.sum(wide * wide, axis=0, keepdims=True) * scale
    high = norm.astype(BF16).astype(F32)
    rest = norm - high
    middle = rest.astype(BF16).astype(F32)
    return high, middle, rest - middle


def lifted(points, left):
    dim, count = points.shape
    scale = math.log2(math.e) / dim
    wide = points.astype(F32)
    high, middle, low = split_norm(wide, -scale)
    row = lax.broadcasted_iota(jnp.int32, (16, count), 0)
    at = 0 if left else 3
    ones = 3 - at
    extra = jnp.where(row == at, high, jnp.where(row == at + 1, middle, jnp.where(row == at + 2, low, 0.0)))
    extra = jnp.where((row >= ones) & (row < ones + 3), 1.0, extra).astype(BF16)
    if left:
        scaled = wide * (2.0 * scale)
        first = scaled.astype(BF16)
        second = (scaled - first.astype(F32)).astype(BF16)
    else:
        first = second = points
    return jnp.concatenate([first, second, extra], axis=0)


def gaussian(left, right):
    return jnp.exp2(dot(left, right, ((0,), (0,)))).astype(BF16)


def call(body, name, outs, args, flops, smem=(), scratch=(), in_specs=None, after=(), out_space=pltpu.VMEM):
    specs = in_specs or [pl.BlockSpec(memory_space=pltpu.SMEM if k in smem else pltpu.VMEM) for k in range(len(args))]
    specs = specs + [pl.BlockSpec(memory_space=pl.ANY) for _ in after]
    taken = len(args)

    def reading(*refs):
        body(*refs[:taken], *refs[taken + len(after) :])

    moved = sum(a.size * a.dtype.itemsize for a in args) + sum(math.prod(s) * jnp.dtype(t).itemsize for s, t in outs)
    return pl.pallas_call(
        reading,
        name=name,
        in_specs=specs,
        out_specs=[pl.BlockSpec(memory_space=out_space) for _ in outs],
        out_shape=[jax.ShapeDtypeStruct(s, t) for s, t in outs],
        scratch_shapes=list(scratch),
        compiler_params=pltpu.CompilerParams(vmem_limit_bytes=VMEM_BYTES),
        cost_estimate=pl.CostEstimate(flops=int(flops * WORK), bytes_accessed=int(moved * WORK), transcendentals=0),
    )(*args, *after)


def pack(half):
    return jnp.concatenate([half[:32], half[32:]], axis=1)


def unpack(packed):
    return jnp.concatenate([packed[:, :256], packed[:, 256:]], axis=0)


def picked(columns, count, wide, kept):
    source = lax.broadcasted_iota(jnp.int32, (columns.shape[1], count), 0)
    target = lax.broadcasted_iota(jnp.int32, (columns.shape[1], count), 1)
    choice = (source == (target // kept) * wide + target % kept).astype(F32).astype(BF16)
    return dot(columns, choice).astype(BF16)


def start_all(copies):
    for copy in copies:
        copy.start()
    return copies


def wait_all(copies):
    for copy in copies:
        copy.wait()


def pack_kernel(points, weights, out, done):
    half = points.shape[1] // 2
    rows = weights.shape[0]
    quarter = rows // 4
    parts = [(weights.at[k * quarter : (k + 1) * quarter, :], out.at[k * quarter : (k + 1) * quarter, :]) for k in range(4)]
    parts += [(points.at[:, k * half : (k + 1) * half], out.at[rows + k * 64 : rows + k * 64 + 64, :]) for k in range(2)]
    wait_all(start_all([pltpu.make_async_copy(a, b, done.at[k]) for k, (a, b) in enumerate(parts)]))


def terms_kernel(w, interp, transfers, send, keep, lifted_weights, transfer0, p, t, done):
    core, _, _ = place()
    half = p.shape[0] // 2
    first = start_all(
        [
            pltpu.make_async_copy(interp.at[k * half : (k + 1) * half, :], p.at[k * half : (k + 1) * half, :], done.at[k])
            for k in range(2)
        ]
    )
    levels = start_all([pltpu.make_async_copy(transfers.at[0, k + 1], t.at[k], done.at[2 + k]) for k in range(4)])
    last = start_all([pltpu.make_async_copy(transfers.at[0, 0], transfer0, done.at[6])])
    wait_all(first)
    lifted_weights[...] = dot(w[0 : 2 * half, :], p[...], ((0,), (0,))).astype(BF16)
    theirs = pl.multiple_of((1 - core) * 256, 256)
    mine = pl.multiple_of(core * 256, 256)
    for k in range(4):
        levels[k].wait()
        send[k * 256 : (k + 1) * 256, :] = dot(lifted_weights[pl.ds(theirs, 256), :], t[k]).astype(BF16)
        keep[k * 256 : (k + 1) * 256, :] = dot(lifted_weights[pl.ds(mine, 256), :], t[k])
    wait_all(last)


def leaf_kernel(lifted_weights, t, payload, index, out):
    size = payload.shape[0] - 128
    out[0:512, :] = dot(lifted_weights[...], t[...]).astype(BF16)
    rank = lax.broadcasted_iota(jnp.int32, (size // 2, index.shape[1]), 0)
    chosen = dot(payload[size : size + 64, :], (rank == index[...]).astype(F32).astype(BF16))
    chosen = chosen + dot(payload[size + 64 : size + 128, :], (rank + size // 2 == index[...]).astype(F32).astype(BF16))
    out[512:576, :] = chosen.astype(BF16)


def chip_kernel(keep, came, mine, theirs, to2, to4, to6, kept, pair, total):
    core, x, _ = place()
    mine, theirs = mine[512:576, :], theirs[512:576, :]
    first = jnp.where(core == 0, mine, theirs)
    second = jnp.where(core == 0, theirs, mine)
    pair[0:64, :] = first
    pair[64:128, :] = second
    total[...] = keep[...] + came[...].astype(F32)
    to2[192:448, :] = total[0:256, :].astype(BF16)
    to2[128:192, :] = jnp.concatenate([first[:, :256], second[:, :256]], axis=1)
    for level, at in ((3, 0), (4, 64)):
        for out, row, other in ((to2, 0, x ^ 1), (to4, 128, x ^ 2), (to6, 128, x ^ 3)):
            rows = pl.ds(pl.multiple_of((level - 1) * 256 + other * 64, 64), 64)
            out[row + at : row + at + 64, :] = total[rows, :].astype(BF16)
        kept[at : at + 64, :] = total[pl.ds(pl.multiple_of((level - 1) * 256 + x * 64, 64), 64), :]
    packed = pack(jnp.concatenate([first[:, :128], second[:, :128]], axis=1))
    for out, part in ((to4, x & 1), (to6, (x & 1) ^ 1)):
        out[0:128, :] = total[pl.ds(pl.multiple_of(256 + part * 128, 128), 128), :].astype(BF16)
        out[256:288, :] = packed


def row_kernel(from2, from4, from6, kept, pair, to8, to16, ring):
    _, x, _ = place()
    near = from2[128:192, :]
    ring[x] = jnp.concatenate([pair[0:64, 0:128], pair[64:128, 0:128]], axis=1)
    ring[x ^ 1] = jnp.concatenate([near[:, 0:128], near[:, 256:384]], axis=1)
    ring[x ^ 2] = unpack(from4[256:288, :])
    ring[x ^ 3] = unpack(from6[256:288, :])
    points3 = picked(jnp.concatenate([ring[k] for k in range(4)], axis=1), 512, 128, 64)
    for out, at in ((to8, 0), (to16, 64)):
        total = kept[at : at + 64, :] + from2[at : 64 + at, :].astype(F32)
        total = total + from4[128 + at : 192 + at, :].astype(F32) + from6[128 + at : 192 + at, :].astype(F32)
        out[0:64, :] = total.astype(BF16)
    to8[64:128, :] = points3
    to16[64:96, :] = pack(picked(points3, 256, 64, 32))


def couple(sums, own, sibling):
    return dot(sums, gaussian(lifted(sibling, True), lifted(own, False))).astype(BF16)


def couple_low_kernel(term0, from2, from4, from6, pair, ring, out0, out1, out2):
    core, x, _ = place()
    first, second = pair[0:64, :], pair[64:128, :]
    out0[...] = couple(term0[0:512, :], jnp.where(core == 0, first, second), jnp.where(core == 0, second, first))
    own = jnp.concatenate([first[:, 0:256], second[:, 0:256]], axis=1)
    out1[...] = couple(from2[192:448, :], own, from2[128:192, :])
    low = x & 2
    own = jnp.concatenate([ring[low], ring[low | 1]], axis=1)
    sibling = jnp.concatenate([ring[low ^ 2], ring[(low ^ 2) | 1]], axis=1)
    sums = (from4[0:128, :].astype(F32) + from6[0:128, :].astype(F32)).astype(BF16)
    out2[...] = couple(sums, own, sibling)


def couple_high_kernel(from8, from16, from24, to8, to16, coupled2, out2, out4):
    _, _, z = place()
    points3 = from8[64:128, :]
    level3 = couple(from8[0:64, :], to8[64:128, :], points3)
    mine, beside = unpack(to16[64:96, :]), picked(points3, 256, 64, 32)
    even = (z & 1) == 0
    own = jnp.concatenate([jnp.where(even, mine, beside), jnp.where(even, beside, mine)], axis=1)
    across, past = unpack(from16[64:96, :]), unpack(from24[64:96, :])
    sibling = jnp.concatenate([jnp.where(even, across, past), jnp.where(even, past, across)], axis=1)
    sums = (from16[0:64, :].astype(F32) + from24[0:64, :].astype(F32)).astype(BF16)
    level4 = couple(sums, own, sibling)
    out2[0:64, :] = level3
    out2[64:128, :] = level4
    out2[128:256, :] = coupled2[...]
    out4[0:64, :] = level3
    out4[64:128, :] = level4


def half_kernel(coupled1, own, from2, from4, from6, out):
    _, x, _ = place()
    out[0:256, :] = coupled1[...]
    out[pl.ds(pl.multiple_of(256 + (x & 1) * 128, 128), 128), :] = own[128:256, :]
    out[pl.ds(pl.multiple_of(256 + ((x & 1) ^ 1) * 128, 128), 128), :] = from2[128:256, :]
    for base, at in ((512, 0), (768, 64)):
        for part, block in ((x, own), (x ^ 1, from2), (x ^ 2, from4), (x ^ 3, from6)):
            out[pl.ds(pl.multiple_of(base + part * 64, 64), 64), :] = block[at : at + 64, :]


def near_kernel(count, slots, with_total, *refs):
    mask, own = refs[0], refs[1]
    blocks = refs[2 : 2 + count]
    total = refs[2 + count] if with_total else None
    out, token = refs[-2], refs[-1]
    token[...] = jnp.zeros_like(token)
    core, _, _ = place()
    size = own.shape[1]
    left = lifted(own[...], True)
    result = [None] * (size // ROWS)
    for block, slot in zip(blocks, slots):
        if slot is None:
            right = lifted(own[...], False)
        else:
            columns = jnp.concatenate([block[size : size + 64, :], block[size + 64 : size + 128, :]], axis=1)
            right = lifted(columns, False)
            flag = jnp.where(core == 0, mask[0, slot[0]], mask[0, slot[1]]).astype(F32)
        values = block[0:size, :]
        for k in range(size // ROWS):
            tile = gaussian(left[:, k * ROWS : (k + 1) * ROWS], right)
            part = dot(tile, values)
            if slot is not None:
                part = part * flag
            result[k] = part if result[k] is None else result[k] + part
    for k in range(size // ROWS):
        rows = slice(k * ROWS, (k + 1) * ROWS)
        out[rows, :] = result[k] + total[rows, :] if with_total else result[k]


def near(mask, points, blocks, slots, total, name, after, cover=1):
    args = [mask, points, *blocks] + ([] if total is None else [total])
    size, width = points.shape[1], blocks[0].shape[1]

    def body(*refs):
        near_kernel(len(blocks), slots, total is not None, *refs)

    flops = cover * 2 * len(blocks) * size * size * (width + 256)
    return call(body, name, [((size, width), F32), ((8, 128), F32)], args, flops, smem=(0,), after=after)


def add_levels(far, transfers, half, part):
    columns = pl.ds(pl.multiple_of(part * 256, 256), 256)
    value = far[:, columns]
    for level in range(1, 5):
        value = value + dot(transfers[0, level], half[(level - 1) * 256 : level * 256, :], ((1,), (1,)))
    far[:, columns] = value


def far_kernel(transfers, coupled0, mine, far):
    core, _, _ = place()
    far[...] = dot(transfers[0, 0], coupled0[...], ((1,), (1,)))
    add_levels(far, transfers, mine, core)


def product_kernel(total, interp, transfers, begun, theirs, product, far, out, done):
    core, _, _ = place()
    far[...] = begun[...]
    add_levels(far, transfers, theirs, 1 - core)
    skeleton = far[...].astype(BF16)
    copies = []
    for k in range(total.shape[0] // 128):
        rows = slice(k * 128, (k + 1) * 128)
        out[rows, :] = (total[rows, :] + dot(interp[rows, :], skeleton)).astype(BF16)
        copies += start_all([pltpu.make_async_copy(out.at[rows, :], product.at[rows, :], done.at[k])])
    wait_all(copies)


def per_device(points, weights, interp, transfers, near_mask, skel_index):
    leaves = lax.axis_size(AXIS)
    size, width = weights.shape

    def swap(value, mask):
        return lax.ppermute(value, AXIS, [(leaf, leaf ^ mask) for leaf in range(leaves)])

    def moved(value, even, odd):
        pairs = [(leaf, leaf + (odd if leaf & 1 else even)) for leaf in range(leaves)]
        return lax.ppermute(value, AXIS, [(a, b) for a, b in pairs if 0 <= b < leaves])

    def staged_across_rows(value):
        end = {leaf: leaf + (-8 if leaf & 1 else 8) for leaf in range(leaves) if (leaf & 7) in (1, 6)}
        pairs = [(leaf, end.get(leaf, leaf)) for leaf in range(leaves)]
        return lax.ppermute(value, AXIS, [(a, b) for a, b in pairs if 0 <= b < leaves])

    def turned(value):
        pairs = [(leaf, (leaf & ~7) | ((leaf + (-2 if leaf & 1 else 2)) & 7)) for leaf in range(leaves)]
        return lax.ppermute(value, AXIS, pairs)

    def rows(count, dtype=BF16):
        return (count, 512), dtype

    def near_of(blocks, slots, total, name, after, cover=1):
        return near(near_mask, points, blocks, slots, total, name, after, cover)

    in_hbm = pl.BlockSpec(memory_space=pltpu.HBM)

    def kept_in_hbm(value):
        return pltpu.with_memory_space_constraint(value, pltpu.HBM)

    in_vmem = pl.BlockSpec(memory_space=pltpu.VMEM)
    (payload,) = call(
        pack_kernel,
        "pack",
        [rows(size + 128)],
        [kept_in_hbm(points), kept_in_hbm(weights)],
        0,
        scratch=[pltpu.SemaphoreType.DMA((6,))],
        in_specs=[in_hbm] * 2,
    )
    outer = moved(payload, -1, 1)
    partner = swap(payload, 1)
    send, keep, lifted_weights, transfer0 = call(
        terms_kernel,
        "terms",
        [rows(1024), rows(1024, F32), rows(512), rows(512)],
        [payload, kept_in_hbm(interp), kept_in_hbm(transfers)],
        2 * 512 * 512 * (1024 + 4 * 512),
        scratch=[
            pltpu.VMEM((size, 512), BF16),
            pltpu.VMEM((4, 512, 512), BF16),
            pltpu.SemaphoreType.DMA((7,)),
        ],
        in_specs=[in_vmem, in_hbm, in_hbm],
    )
    came = swap(send, 1)
    (term0,) = call(
        leaf_kernel,
        "leaf",
        [rows(576)],
        [lifted_weights, transfer0, payload, skel_index],
        2 * 512 * 512 * 768,
    )
    other0 = swap(term0, 1)
    total, token = near_of([payload, partner], [None, (2, 1)], None, "near_own", (term0,), cover=20)

    to2, to4, to6, kept, pair = call(
        chip_kernel,
        "chip",
        [rows(448), rows(288), rows(288), rows(128, F32), rows(128)],
        [keep, came, term0, other0],
        1e6,
        after=(token,),
        scratch=[pltpu.VMEM((1024, 512), F32)],
    )
    from2, from4, from6 = swap(to2, 2), swap(to4, 4), swap(to6, 6)
    late, pair = lax.optimization_barrier((payload, pair))
    staged = staged_across_rows(late)
    total, token = near_of([outer], [(1, 2)], total, "near_outer", (pair,))

    to8, to16, ring = call(
        row_kernel,
        "row",
        [rows(128), rows(96), ((4, 64, 256), BF16)],
        [from2, from4, from6, kept, pair],
        1e8,
        after=(token,),
    )
    staged, outer, ring = lax.optimization_barrier((staged, outer, ring))
    second = turned(staged)
    past = swap(outer, 1)
    from8, from16, from24 = swap(to8, 8), swap(to16, 16), swap(to16, 24)
    coupled0, coupled1, coupled2 = call(
        couple_low_kernel,
        "couple_low",
        [rows(512), rows(256), rows(128)],
        [other0, from2, from4, from6, pair, ring],
        1e6,
    )
    total, token = near_of([past], [(3, 0)], total, "near_past", (coupled2,), cover=0.01)
    part2, part4 = call(
        couple_high_kernel,
        "couple_high",
        [rows(256), rows(128)],
        [from8, from16, from24, to8, to16, coupled2],
        1e6,
        after=(token,),
    )
    back2, back4, back6 = swap(part2, 2), swap(part4, 4), swap(part4, 6)
    total, token = near_of([second], [(0, 3)], total, "near_second", (part4,))
    (mine,) = call(
        half_kernel, "half", [rows(1024)], [coupled1, part2, back2, back4, back6], 1e6, after=(token,)
    )
    theirs = swap(mine, 1)
    (far,) = call(far_kernel, "far", [rows(512, F32)], [transfers, coupled0, mine], 2 * 512 * 512 * 5 * 400)
    return call(
        product_kernel,
        "product",
        [((size, width), BF16)],
        [total, interp, transfers, far, theirs],
        2 * 512 * 512 * (4 * 256 + 1024),
        scratch=[
            pltpu.VMEM((512, 512), F32),
            pltpu.VMEM((size, width), BF16),
            pltpu.SemaphoreType.DMA((size // 128,)),
        ],
        out_space=pltpu.HBM,
    )[0]


def solution(mesh):
    return jax.shard_map(
        per_device,
        mesh=mesh,
        in_specs=(
            P(None, AXIS),
            P(AXIS, None),
            P(AXIS, None),
            P(AXIS, None, None, None),
            P(AXIS, None),
            P(AXIS, None),
        ),
        out_specs=P(AXIS, None),
        check_vma=False,
    )
```

```python
import math

import jax
import jax.numpy as jnp
from jax import lax
from jax.experimental import pallas as pl
from jax.experimental.pallas import tpu as pltpu
from jax.sharding import PartitionSpec as P

F32 = jnp.float32
BF16 = jnp.bfloat16
AXIS = "leaf"
VMEM_BYTES = 24 * 1024 * 1024
ROWS = 256
WORK = 1.0
LOW = 1.0


def dot(a, b, over=((1,), (0,))):
    return lax.dot_general(a, b, (over, ((), ())), preferred_element_type=F32)


def place():
    leaf = lax.axis_index(AXIS)
    return leaf & 1, (leaf >> 1) & 3, (leaf >> 3) & 3


def split_norm(wide, scale):
    norm = jnp.sum(wide * wide, axis=0, keepdims=True) * scale
    high = norm.astype(BF16).astype(F32)
    rest = norm - high
    middle = rest.astype(BF16).astype(F32)
    return high, middle, rest - middle


def lifted(points, left):
    dim, count = points.shape
    scale = math.log2(math.e) / dim
    wide = points.astype(F32)
    high, middle, low = split_norm(wide, -scale)
    row = lax.broadcasted_iota(jnp.int32, (16, count), 0)
    at = 0 if left else 3
    ones = 3 - at
    extra = jnp.where(row == at, high, jnp.where(row == at + 1, middle, jnp.where(row == at + 2, low, 0.0)))
    extra = jnp.where((row >= ones) & (row < ones + 3), 1.0, extra).astype(BF16)
    if left:
        scaled = wide * (2.0 * scale)
        first = scaled.astype(BF16)
        second = (scaled - first.astype(F32)).astype(BF16)
    else:
        first = second = points
    return jnp.concatenate([first, second, extra], axis=0)


def gaussian(left, right):
    return jnp.exp2(dot(left, right, ((0,), (0,)))).astype(BF16)


def call(body, name, outs, args, flops, smem=(), scratch=(), in_specs=None, after=(), out_space=pltpu.VMEM):
    specs = in_specs or [pl.BlockSpec(memory_space=pltpu.SMEM if k in smem else pltpu.VMEM) for k in range(len(args))]
    specs = specs + [pl.BlockSpec(memory_space=pl.ANY) for _ in after]
    taken = len(args)

    def reading(*refs):
        body(*refs[:taken], *refs[taken + len(after) :])

    moved = sum(a.size * a.dtype.itemsize for a in args) + sum(math.prod(s) * jnp.dtype(t).itemsize for s, t in outs)
    return pl.pallas_call(
        reading,
        name=name,
        in_specs=specs,
        out_specs=[pl.BlockSpec(memory_space=out_space) for _ in outs],
        out_shape=[jax.ShapeDtypeStruct(s, t) for s, t in outs],
        scratch_shapes=list(scratch),
        compiler_params=pltpu.CompilerParams(vmem_limit_bytes=VMEM_BYTES),
        cost_estimate=pl.CostEstimate(flops=int(flops * WORK), bytes_accessed=int(moved * WORK), transcendentals=0),
    )(*args, *after)


def pack(half):
    return jnp.concatenate([half[:32], half[32:]], axis=1)


def unpack(packed):
    return jnp.concatenate([packed[:, :256], packed[:, 256:]], axis=0)


def picked(columns, count, wide, kept):
    source = lax.broadcasted_iota(jnp.int32, (columns.shape[1], count), 0)
    target = lax.broadcasted_iota(jnp.int32, (columns.shape[1], count), 1)
    choice = (source == (target // kept) * wide + target % kept).astype(F32).astype(BF16)
    return dot(columns, choice).astype(BF16)


def start_all(copies):
    for copy in copies:
        copy.start()
    return copies


def wait_all(copies):
    for copy in copies:
        copy.wait()


def pack_kernel(points, weights, out, done):
    half = points.shape[1] // 2
    rows = weights.shape[0]
    quarter = rows // 4
    parts = [(weights.at[k * quarter : (k + 1) * quarter, :], out.at[k * quarter : (k + 1) * quarter, :]) for k in range(4)]
    parts += [(points.at[:, k * half : (k + 1) * half], out.at[rows + k * 64 : rows + k * 64 + 64, :]) for k in range(2)]
    wait_all(start_all([pltpu.make_async_copy(a, b, done.at[k]) for k, (a, b) in enumerate(parts)]))


def terms_kernel(w, p, transfers, send, keep, lifted_weights, transfer0, t, done):
    core, _, _ = place()
    levels = start_all([pltpu.make_async_copy(transfers.at[0, k + 1], t.at[k], done.at[k]) for k in range(4)])
    last = start_all([pltpu.make_async_copy(transfers.at[0, 0], transfer0, done.at[4])])
    lifted_weights[...] = dot(w[0 : p.shape[0], :], p[...], ((0,), (0,))).astype(BF16)
    theirs = pl.multiple_of((1 - core) * 256, 256)
    mine = pl.multiple_of(core * 256, 256)
    for k in range(4):
        levels[k].wait()
        send[k * 256 : (k + 1) * 256, :] = dot(lifted_weights[pl.ds(theirs, 256), :], t[k]).astype(BF16)
        keep[k * 256 : (k + 1) * 256, :] = dot(lifted_weights[pl.ds(mine, 256), :], t[k])
    wait_all(last)


def leaf_kernel(lifted_weights, t, payload, index, out):
    size = payload.shape[0] - 128
    out[0:512, :] = dot(lifted_weights[...], t[...]).astype(BF16)
    rank = lax.broadcasted_iota(jnp.int32, (size // 2, index.shape[1]), 0)
    chosen = dot(payload[size : size + 64, :], (rank == index[...]).astype(F32).astype(BF16))
    chosen = chosen + dot(payload[size + 64 : size + 128, :], (rank + size // 2 == index[...]).astype(F32).astype(BF16))
    out[512:576, :] = chosen.astype(BF16)


def chip_kernel(keep, came, mine, theirs, to2, to4, to6, kept, pair, total):
    core, x, _ = place()
    mine, theirs = mine[512:576, :], theirs[512:576, :]
    first = jnp.where(core == 0, mine, theirs)
    second = jnp.where(core == 0, theirs, mine)
    pair[0:64, :] = first
    pair[64:128, :] = second
    total[...] = keep[...] + came[...].astype(F32)
    to2[192:448, :] = total[0:256, :].astype(BF16)
    to2[128:192, :] = jnp.concatenate([first[:, :256], second[:, :256]], axis=1)
    for level, at in ((3, 0), (4, 64)):
        for out, row, other in ((to2, 0, x ^ 1), (to4, 128, x ^ 2), (to6, 128, x ^ 3)):
            rows = pl.ds(pl.multiple_of((level - 1) * 256 + other * 64, 64), 64)
            out[row + at : row + at + 64, :] = total[rows, :].astype(BF16)
        kept[at : at + 64, :] = total[pl.ds(pl.multiple_of((level - 1) * 256 + x * 64, 64), 64), :]
    packed = pack(jnp.concatenate([first[:, :128], second[:, :128]], axis=1))
    for out, part in ((to4, x & 1), (to6, (x & 1) ^ 1)):
        out[0:128, :] = total[pl.ds(pl.multiple_of(256 + part * 128, 128), 128), :].astype(BF16)
        out[256:288, :] = packed


def row_kernel(from2, from4, from6, kept, pair, to8, to16, ring):
    _, x, _ = place()
    near = from2[128:192, :]
    ring[x] = jnp.concatenate([pair[0:64, 0:128], pair[64:128, 0:128]], axis=1)
    ring[x ^ 1] = jnp.concatenate([near[:, 0:128], near[:, 256:384]], axis=1)
    ring[x ^ 2] = unpack(from4[256:288, :])
    ring[x ^ 3] = unpack(from6[256:288, :])
    points3 = picked(jnp.concatenate([ring[k] for k in range(4)], axis=1), 512, 128, 64)
    for out, at in ((to8, 0), (to16, 64)):
        total = kept[at : at + 64, :] + from2[at : 64 + at, :].astype(F32)
        total = total + from4[128 + at : 192 + at, :].astype(F32) + from6[128 + at : 192 + at, :].astype(F32)
        out[0:64, :] = total.astype(BF16)
    to8[64:128, :] = points3
    to16[64:96, :] = pack(picked(points3, 256, 64, 32))


def couple(sums, own, sibling):
    return dot(sums, gaussian(lifted(sibling, True), lifted(own, False))).astype(BF16)


def couple_low_kernel(term0, from2, from4, from6, pair, ring, out0, out1, out2):
    core, x, _ = place()
    first, second = pair[0:64, :], pair[64:128, :]
    out0[...] = couple(term0[0:512, :], jnp.where(core == 0, first, second), jnp.where(core == 0, second, first))
    own = jnp.concatenate([first[:, 0:256], second[:, 0:256]], axis=1)
    out1[...] = couple(from2[192:448, :], own, from2[128:192, :])
    low = x & 2
    own = jnp.concatenate([ring[low], ring[low | 1]], axis=1)
    sibling = jnp.concatenate([ring[low ^ 2], ring[(low ^ 2) | 1]], axis=1)
    sums = (from4[0:128, :].astype(F32) + from6[0:128, :].astype(F32)).astype(BF16)
    out2[...] = couple(sums, own, sibling)


def couple_high_kernel(from8, from16, from24, to8, to16, coupled2, out2, out4):
    _, _, z = place()
    points3 = from8[64:128, :]
    level3 = couple(from8[0:64, :], to8[64:128, :], points3)
    mine, beside = unpack(to16[64:96, :]), picked(points3, 256, 64, 32)
    even = (z & 1) == 0
    own = jnp.concatenate([jnp.where(even, mine, beside), jnp.where(even, beside, mine)], axis=1)
    across, past = unpack(from16[64:96, :]), unpack(from24[64:96, :])
    sibling = jnp.concatenate([jnp.where(even, across, past), jnp.where(even, past, across)], axis=1)
    sums = (from16[0:64, :].astype(F32) + from24[0:64, :].astype(F32)).astype(BF16)
    level4 = couple(sums, own, sibling)
    out2[0:64, :] = level3
    out2[64:128, :] = level4
    out2[128:256, :] = coupled2[...]
    out4[0:64, :] = level3
    out4[64:128, :] = level4


def half_kernel(coupled1, own, from2, from4, from6, out):
    _, x, _ = place()
    out[0:256, :] = coupled1[...]
    out[pl.ds(pl.multiple_of(256 + (x & 1) * 128, 128), 128), :] = own[128:256, :]
    out[pl.ds(pl.multiple_of(256 + ((x & 1) ^ 1) * 128, 128), 128), :] = from2[128:256, :]
    for base, at in ((512, 0), (768, 64)):
        for part, block in ((x, own), (x ^ 1, from2), (x ^ 2, from4), (x ^ 3, from6)):
            out[pl.ds(pl.multiple_of(base + part * 64, 64), 64), :] = block[at : at + 64, :]


def near_kernel(count, slots, with_total, *refs):
    mask, own = refs[0], refs[1]
    blocks = refs[2 : 2 + count]
    total = refs[2 + count] if with_total else None
    out, token = refs[-2], refs[-1]
    token[...] = jnp.zeros_like(token)
    core, _, _ = place()
    size = own.shape[1]
    left = lifted(own[...], True)
    result = [None] * (size // ROWS)
    for block, slot in zip(blocks, slots):
        if slot is None:
            right = lifted(own[...], False)
        else:
            columns = jnp.concatenate([block[size : size + 64, :], block[size + 64 : size + 128, :]], axis=1)
            right = lifted(columns, False)
            flag = jnp.where(core == 0, mask[0, slot[0]], mask[0, slot[1]]).astype(F32)
        values = block[0:size, :]
        for k in range(size // ROWS):
            tile = gaussian(left[:, k * ROWS : (k + 1) * ROWS], right)
            part = dot(tile, values)
            if slot is not None:
                part = part * flag
            result[k] = part if result[k] is None else result[k] + part
    for k in range(size // ROWS):
        rows = slice(k * ROWS, (k + 1) * ROWS)
        out[rows, :] = result[k] + total[rows, :] if with_total else result[k]


def near(mask, points, blocks, slots, total, name, after, cover=1):
    args = [mask, points, *blocks] + ([] if total is None else [total])
    size, width = points.shape[1], blocks[0].shape[1]

    def body(*refs):
        near_kernel(len(blocks), slots, total is not None, *refs)

    flops = cover * 2 * len(blocks) * size * size * (width + 256)
    return call(body, name, [((size, width), F32), ((8, 128), F32)], args, flops, smem=(0,), after=after)


def columns_of(core):
    return pl.ds(pl.multiple_of(core * 256, 256), 256)


def with_levels(value, transfers, half):
    for level in range(1, 5):
        value = value + dot(transfers[0, level], half[(level - 1) * 256 : level * 256, :], ((1,), (1,)))
    return value


def far_kernel(transfers, coupled0, mine, total, interp, begun, out):
    core, _, _ = place()
    begun[...] = dot(transfers[0, 0], coupled0[...], ((1,), (1,)))
    columns = columns_of(core)
    skeleton = with_levels(begun[:, columns], transfers, mine).astype(BF16)
    block = total.shape[0] // 2
    for k in range(2):
        rows = slice(k * block, (k + 1) * block)
        out[rows, :] = (total[rows, columns] + dot(interp[rows, :], skeleton)).astype(BF16)


def product_kernel(total, interp, transfers, begun, theirs, ready, product, out, done):
    core, _, _ = place()
    columns = columns_of(1 - core)
    out[:, columns_of(core)] = ready[...]
    skeleton = with_levels(begun[:, columns], transfers, theirs).astype(BF16)
    copies = []
    block = total.shape[0] // 2
    for k in range(2):
        rows = slice(k * block, (k + 1) * block)
        out[rows, columns] = (total[rows, columns] + dot(interp[rows, :], skeleton)).astype(BF16)
        copies += start_all(
            [
                pltpu.make_async_copy(out.at[pl.ds(at, 128), :], product.at[pl.ds(at, 128), :], done.at[at // 128])
                for at in range(k * block, (k + 1) * block, 128)
            ]
        )
    wait_all(copies)


def per_device(points, weights, interp, transfers, near_mask, skel_index):
    leaves = lax.axis_size(AXIS)
    size, width = weights.shape

    def swap(value, mask):
        return lax.ppermute(value, AXIS, [(leaf, leaf ^ mask) for leaf in range(leaves)])

    def moved(value, even, odd):
        pairs = [(leaf, leaf + (odd if leaf & 1 else even)) for leaf in range(leaves)]
        return lax.ppermute(value, AXIS, [(a, b) for a, b in pairs if 0 <= b < leaves])

    def staged_across_rows(value):
        end = {leaf: leaf + (-8 if leaf & 1 else 8) for leaf in range(leaves) if (leaf & 7) in (1, 6)}
        pairs = [(leaf, end.get(leaf, leaf)) for leaf in range(leaves)]
        return lax.ppermute(value, AXIS, [(a, b) for a, b in pairs if 0 <= b < leaves])

    def turned(value):
        pairs = [(leaf, (leaf & ~7) | ((leaf + (-2 if leaf & 1 else 2)) & 7)) for leaf in range(leaves)]
        return lax.ppermute(value, AXIS, pairs)

    def rows(count, dtype=BF16):
        return (count, 512), dtype

    def near_of(blocks, slots, total, name, after, cover=1):
        return near(near_mask, points, blocks, slots, total, name, after, cover)

    in_hbm = pl.BlockSpec(memory_space=pltpu.HBM)

    def kept_in_hbm(value):
        return pltpu.with_memory_space_constraint(value, pltpu.HBM)

    in_vmem = pl.BlockSpec(memory_space=pltpu.VMEM)
    (payload,) = call(
        pack_kernel,
        "pack",
        [rows(size + 128)],
        [kept_in_hbm(points), kept_in_hbm(weights)],
        0,
        scratch=[pltpu.SemaphoreType.DMA((6,))],
        in_specs=[in_hbm] * 2,
    )
    outer = moved(payload, -1, 1)
    partner = swap(payload, 1)
    send, keep, lifted_weights, transfer0 = call(
        terms_kernel,
        "terms",
        [rows(1024), rows(1024, F32), rows(512), rows(512)],
        [payload, interp, kept_in_hbm(transfers)],
        2 * 512 * 512 * (1024 + 4 * 512),
        scratch=[
            pltpu.VMEM((4, 512, 512), BF16),
            pltpu.SemaphoreType.DMA((5,)),
        ],
        in_specs=[in_vmem, in_vmem, in_hbm],
    )
    came = swap(send, 1)
    (term0,) = call(
        leaf_kernel,
        "leaf",
        [rows(576)],
        [lifted_weights, transfer0, payload, skel_index],
        2 * 512 * 512 * 768,
    )
    other0 = swap(term0, 1)
    total, token = near_of([payload], [None], None, "near_self", (term0,), cover=20)

    to2, to4, to6, kept, pair = call(
        chip_kernel,
        "chip",
        [rows(448), rows(288), rows(288), rows(128, F32), rows(128)],
        [keep, came, term0, other0],
        1e6,
        after=(token, partner),
        scratch=[pltpu.VMEM((1024, 512), F32)],
    )
    from2, from4, from6 = swap(to2, 2), swap(to4, 4), swap(to6, 6)
    late, pair = lax.optimization_barrier((payload, pair))
    staged = staged_across_rows(late)
    total, token = near_of([partner, outer], [(2, 1), (1, 2)], total, "near_one", (pair,))

    to8, to16, ring = call(
        row_kernel,
        "row",
        [rows(128), rows(96), ((4, 64, 256), BF16)],
        [from2, from4, from6, kept, pair],
        1e8,
        after=(token,),
    )
    staged, outer, ring = lax.optimization_barrier((staged, outer, ring))
    second = turned(staged)
    past = swap(outer, 1)
    from8, from16, from24 = swap(to8, 8), swap(to16, 16), swap(to16, 24)
    coupled0, coupled1, coupled2 = call(
        couple_low_kernel,
        "couple_low",
        [rows(512), rows(256), rows(128)],
        [other0, from2, from4, from6, pair, ring],
        1e6,
    )
    total, token = near_of([past], [(3, 0)], total, "near_past", (coupled2,), cover=0.01)
    part2, part4 = call(
        couple_high_kernel,
        "couple_high",
        [rows(256), rows(128)],
        [from8, from16, from24, to8, to16, coupled2],
        1e6,
        after=(token,),
    )
    back2, back4, back6 = swap(part2, 2), swap(part4, 4), swap(part4, 6)
    total, token = near_of([second], [(0, 3)], total, "near_second", (part4,))
    (mine,) = call(
        half_kernel, "half", [rows(1024)], [coupled1, part2, back2, back4, back6], 1e6, after=(token,)
    )
    theirs = swap(mine, 1)
    far, ready = call(
        far_kernel,
        "far",
        [rows(512, F32), ((size, 256), BF16)],
        [transfers, coupled0, mine, total, interp],
        2 * 512 * 512 * (512 + 4 * 256 + 512),
    )
    return call(
        product_kernel,
        "product",
        [((size, width), BF16)],
        [total, interp, transfers, far, theirs, ready],
        2 * 512 * 512 * (4 * 256 + 512),
        scratch=[pltpu.VMEM((size, width), BF16), pltpu.SemaphoreType.DMA((size // 128,))],
        out_space=pltpu.HBM,
    )[0]


def solution(mesh):
    return jax.shard_map(
        per_device,
        mesh=mesh,
        in_specs=(
            P(None, AXIS),
            P(AXIS, None),
            P(AXIS, None),
            P(AXIS, None, None, None),
            P(AXIS, None),
            P(AXIS, None),
        ),
        out_specs=P(AXIS, None),
        check_vma=False,
    )
```

```python
import math

import jax
import jax.numpy as jnp
from jax import lax
from jax.experimental import pallas as pl
from jax.experimental.pallas import tpu as pltpu
from jax.sharding import PartitionSpec as P

F32 = jnp.float32
BF16 = jnp.bfloat16
AXIS = "leaf"
VMEM_BYTES = 24 * 1024 * 1024
ROWS = 256
WORK = 1.0
LOW = 1.0


def dot(a, b, over=((1,), (0,))):
    return lax.dot_general(a, b, (over, ((), ())), preferred_element_type=F32)


def place():
    leaf = lax.axis_index(AXIS)
    return leaf & 1, (leaf >> 1) & 3, (leaf >> 3) & 3


def split_norm(wide, scale):
    norm = jnp.sum(wide * wide, axis=0, keepdims=True) * scale
    high = norm.astype(BF16).astype(F32)
    rest = norm - high
    middle = rest.astype(BF16).astype(F32)
    return high, middle, rest - middle


def lifted(points, left):
    dim, count = points.shape
    scale = math.log2(math.e) / dim
    wide = points.astype(F32)
    high, middle, low = split_norm(wide, -scale)
    row = lax.broadcasted_iota(jnp.int32, (16, count), 0)
    at = 0 if left else 3
    ones = 3 - at
    extra = jnp.where(row == at, high, jnp.where(row == at + 1, middle, jnp.where(row == at + 2, low, 0.0)))
    extra = jnp.where((row >= ones) & (row < ones + 3), 1.0, extra).astype(BF16)
    if left:
        scaled = wide * (2.0 * scale)
        first = scaled.astype(BF16)
        second = (scaled - first.astype(F32)).astype(BF16)
    else:
        first = second = points
    return jnp.concatenate([first, second, extra], axis=0)


def gaussian(left, right):
    return jnp.exp2(dot(left, right, ((0,), (0,)))).astype(BF16)


def call(body, name, outs, args, flops, smem=(), scratch=(), in_specs=None, after=(), out_space=pltpu.VMEM):
    specs = in_specs or [pl.BlockSpec(memory_space=pltpu.SMEM if k in smem else pltpu.VMEM) for k in range(len(args))]
    specs = specs + [pl.BlockSpec(memory_space=pl.ANY) for _ in after]
    taken = len(args)

    def reading(*refs):
        body(*refs[:taken], *refs[taken + len(after) :])

    moved = sum(a.size * a.dtype.itemsize for a in args) + sum(math.prod(s) * jnp.dtype(t).itemsize for s, t in outs)
    return pl.pallas_call(
        reading,
        name=name,
        in_specs=specs,
        out_specs=[pl.BlockSpec(memory_space=out_space) for _ in outs],
        out_shape=[jax.ShapeDtypeStruct(s, t) for s, t in outs],
        scratch_shapes=list(scratch),
        compiler_params=pltpu.CompilerParams(vmem_limit_bytes=VMEM_BYTES),
        cost_estimate=pl.CostEstimate(flops=int(flops * WORK), bytes_accessed=int(moved * WORK), transcendentals=0),
    )(*args, *after)


def pack(half):
    return jnp.concatenate([half[:32], half[32:]], axis=1)


def unpack(packed):
    return jnp.concatenate([packed[:, :256], packed[:, 256:]], axis=0)


def picked(columns, count, wide, kept):
    source = lax.broadcasted_iota(jnp.int32, (columns.shape[1], count), 0)
    target = lax.broadcasted_iota(jnp.int32, (columns.shape[1], count), 1)
    choice = (source == (target // kept) * wide + target % kept).astype(F32).astype(BF16)
    return dot(columns, choice).astype(BF16)


def start_all(copies):
    for copy in copies:
        copy.start()
    return copies


def wait_all(copies):
    for copy in copies:
        copy.wait()


def pack_kernel(points, weights, out, done):
    half = points.shape[1] // 2
    rows = weights.shape[0]
    quarter = rows // 4
    parts = [(weights.at[k * quarter : (k + 1) * quarter, :], out.at[k * quarter : (k + 1) * quarter, :]) for k in range(4)]
    parts += [(points.at[:, k * half : (k + 1) * half], out.at[rows + k * 64 : rows + k * 64 + 64, :]) for k in range(2)]
    wait_all(start_all([pltpu.make_async_copy(a, b, done.at[k]) for k, (a, b) in enumerate(parts)]))


def terms_kernel(w, p, index, transfers, send, keep, lifted_weights, t, done):
    core, _, _ = place()
    copies = start_all([pltpu.make_async_copy(transfers.at[0, (k + 1) % 5], t.at[k], done.at[k]) for k in range(5)])
    size = p.shape[0]
    lifted_weights[...] = dot(w[0:size, :], p[...], ((0,), (0,))).astype(BF16)
    rank = lax.broadcasted_iota(jnp.int32, (size // 2, index.shape[1]), 0)
    chosen = dot(w[size : size + 64, :], (rank == index[...]).astype(F32).astype(BF16))
    chosen = chosen + dot(w[size + 64 : size + 128, :], (rank + size // 2 == index[...]).astype(F32).astype(BF16))
    send[1536:1600, :] = chosen.astype(BF16)
    theirs = pl.multiple_of((1 - core) * 256, 256)
    mine = pl.multiple_of(core * 256, 256)
    for k in range(4):
        copies[k].wait()
        send[k * 256 : (k + 1) * 256, :] = dot(lifted_weights[pl.ds(theirs, 256), :], t[k]).astype(BF16)
        keep[k * 256 : (k + 1) * 256, :] = dot(lifted_weights[pl.ds(mine, 256), :], t[k])
    copies[4].wait()
    send[1024:1536, :] = dot(lifted_weights[...], t[4]).astype(BF16)


def chip_kernel(keep, came, sent, to2, to4, to6, kept, pair, total):
    core, x, _ = place()
    mine, theirs = sent[1536:1600, :], came[1536:1600, :]
    first = jnp.where(core == 0, mine, theirs)
    second = jnp.where(core == 0, theirs, mine)
    pair[0:64, :] = first
    pair[64:128, :] = second
    total[...] = keep[...] + came[0:1024, :].astype(F32)
    to2[192:448, :] = total[0:256, :].astype(BF16)
    to2[128:192, :] = jnp.concatenate([first[:, :256], second[:, :256]], axis=1)
    for level, at in ((3, 0), (4, 64)):
        for out, row, other in ((to2, 0, x ^ 1), (to4, 128, x ^ 2), (to6, 128, x ^ 3)):
            rows = pl.ds(pl.multiple_of((level - 1) * 256 + other * 64, 64), 64)
            out[row + at : row + at + 64, :] = total[rows, :].astype(BF16)
        kept[at : at + 64, :] = total[pl.ds(pl.multiple_of((level - 1) * 256 + x * 64, 64), 64), :]
    packed = pack(jnp.concatenate([first[:, :128], second[:, :128]], axis=1))
    for out, part in ((to4, x & 1), (to6, (x & 1) ^ 1)):
        out[0:128, :] = total[pl.ds(pl.multiple_of(256 + part * 128, 128), 128), :].astype(BF16)
        out[256:288, :] = packed


def row_kernel(from2, from4, from6, kept, pair, to8, to16, ring):
    _, x, _ = place()
    near = from2[128:192, :]
    ring[x] = jnp.concatenate([pair[0:64, 0:128], pair[64:128, 0:128]], axis=1)
    ring[x ^ 1] = jnp.concatenate([near[:, 0:128], near[:, 256:384]], axis=1)
    ring[x ^ 2] = unpack(from4[256:288, :])
    ring[x ^ 3] = unpack(from6[256:288, :])
    points3 = picked(jnp.concatenate([ring[k] for k in range(4)], axis=1), 512, 128, 64)
    for out, at in ((to8, 0), (to16, 64)):
        total = kept[at : at + 64, :] + from2[at : 64 + at, :].astype(F32)
        total = total + from4[128 + at : 192 + at, :].astype(F32) + from6[128 + at : 192 + at, :].astype(F32)
        out[0:64, :] = total.astype(BF16)
    to8[64:128, :] = points3
    to16[64:96, :] = pack(picked(points3, 256, 64, 32))


def couple(sums, own, sibling):
    return dot(sums, gaussian(lifted(sibling, True), lifted(own, False))).astype(BF16)


def couple_low_kernel(came, from2, from4, from6, pair, ring, out0, out1, out2):
    core, x, _ = place()
    first, second = pair[0:64, :], pair[64:128, :]
    out0[...] = couple(came[1024:1536, :], jnp.where(core == 0, first, second), jnp.where(core == 0, second, first))
    own = jnp.concatenate([first[:, 0:256], second[:, 0:256]], axis=1)
    out1[...] = couple(from2[192:448, :], own, from2[128:192, :])
    low = x & 2
    own = jnp.concatenate([ring[low], ring[low | 1]], axis=1)
    sibling = jnp.concatenate([ring[low ^ 2], ring[(low ^ 2) | 1]], axis=1)
    sums = (from4[0:128, :].astype(F32) + from6[0:128, :].astype(F32)).astype(BF16)
    out2[...] = couple(sums, own, sibling)


def couple_high_kernel(from8, from16, from24, to8, to16, coupled2, out2, out4):
    _, _, z = place()
    points3 = from8[64:128, :]
    level3 = couple(from8[0:64, :], to8[64:128, :], points3)
    mine, beside = unpack(to16[64:96, :]), picked(points3, 256, 64, 32)
    even = (z & 1) == 0
    own = jnp.concatenate([jnp.where(even, mine, beside), jnp.where(even, beside, mine)], axis=1)
    across, past = unpack(from16[64:96, :]), unpack(from24[64:96, :])
    sibling = jnp.concatenate([jnp.where(even, across, past), jnp.where(even, past, across)], axis=1)
    sums = (from16[0:64, :].astype(F32) + from24[0:64, :].astype(F32)).astype(BF16)
    level4 = couple(sums, own, sibling)
    out2[0:64, :] = level3
    out2[64:128, :] = level4
    out2[128:256, :] = coupled2[...]
    out4[0:64, :] = level3
    out4[64:128, :] = level4


def half_kernel(coupled1, own, from2, from4, from6, out):
    _, x, _ = place()
    out[0:256, :] = coupled1[...]
    out[pl.ds(pl.multiple_of(256 + (x & 1) * 128, 128), 128), :] = own[128:256, :]
    out[pl.ds(pl.multiple_of(256 + ((x & 1) ^ 1) * 128, 128), 128), :] = from2[128:256, :]
    for base, at in ((512, 0), (768, 64)):
        for part, block in ((x, own), (x ^ 1, from2), (x ^ 2, from4), (x ^ 3, from6)):
            out[pl.ds(pl.multiple_of(base + part * 64, 64), 64), :] = block[at : at + 64, :]


def near_kernel(count, slots, with_total, *refs):
    mask, own = refs[0], refs[1]
    blocks = refs[2 : 2 + count]
    total = refs[2 + count] if with_total else None
    out, token = refs[-2], refs[-1]
    token[...] = jnp.zeros_like(token)
    core, _, _ = place()
    size = own.shape[1]
    left = lifted(own[...], True)
    result = [None] * (size // ROWS)
    for block, slot in zip(blocks, slots):
        if slot is None:
            right = lifted(own[...], False)
        else:
            columns = jnp.concatenate([block[size : size + 64, :], block[size + 64 : size + 128, :]], axis=1)
            right = lifted(columns, False)
            flag = jnp.where(core == 0, mask[0, slot[0]], mask[0, slot[1]]).astype(F32)
        values = block[0:size, :]
        for k in range(size // ROWS):
            tile = gaussian(left[:, k * ROWS : (k + 1) * ROWS], right)
            part = dot(tile, values)
            if slot is not None:
                part = part * flag
            result[k] = part if result[k] is None else result[k] + part
    for k in range(size // ROWS):
        rows = slice(k * ROWS, (k + 1) * ROWS)
        out[rows, :] = result[k] + total[rows, :] if with_total else result[k]


def near(mask, points, blocks, slots, total, name, after, cover=1):
    args = [mask, points, *blocks] + ([] if total is None else [total])
    size, width = points.shape[1], blocks[0].shape[1]

    def body(*refs):
        near_kernel(len(blocks), slots, total is not None, *refs)

    flops = cover * 2 * len(blocks) * size * size * (width + 256)
    return call(body, name, [((size, width), F32), ((8, 128), F32)], args, flops, smem=(0,), after=after)


def columns_of(core):
    return pl.ds(pl.multiple_of(core * 256, 256), 256)


def with_levels(value, transfers, half):
    for level in range(1, 5):
        value = value + dot(transfers[0, level], half[(level - 1) * 256 : level * 256, :], ((1,), (1,)))
    return value


def far_kernel(transfers, coupled0, mine, total, interp, begun, out):
    core, _, _ = place()
    begun[...] = dot(transfers[0, 0], coupled0[...], ((1,), (1,)))
    columns = columns_of(core)
    skeleton = with_levels(begun[:, columns], transfers, mine).astype(BF16)
    block = total.shape[0] // 2
    for k in range(2):
        rows = slice(k * block, (k + 1) * block)
        out[rows, :] = (total[rows, columns] + dot(interp[rows, :], skeleton)).astype(BF16)


def product_kernel(total, interp, transfers, begun, theirs, ready, product, out, done):
    core, _, _ = place()
    columns = columns_of(1 - core)
    out[:, columns_of(core)] = ready[...]
    skeleton = with_levels(begun[:, columns], transfers, theirs).astype(BF16)
    copies = []
    block = total.shape[0] // 2
    for k in range(2):
        rows = slice(k * block, (k + 1) * block)
        out[rows, columns] = (total[rows, columns] + dot(interp[rows, :], skeleton)).astype(BF16)
        copies += start_all(
            [
                pltpu.make_async_copy(out.at[pl.ds(at, 128), :], product.at[pl.ds(at, 128), :], done.at[at // 128])
                for at in range(k * block, (k + 1) * block, 128)
            ]
        )
    wait_all(copies)


def per_device(points, weights, interp, transfers, near_mask, skel_index):
    leaves = lax.axis_size(AXIS)
    size, width = weights.shape

    def swap(value, mask):
        return lax.ppermute(value, AXIS, [(leaf, leaf ^ mask) for leaf in range(leaves)])

    def moved(value, even, odd):
        pairs = [(leaf, leaf + (odd if leaf & 1 else even)) for leaf in range(leaves)]
        return lax.ppermute(value, AXIS, [(a, b) for a, b in pairs if 0 <= b < leaves])

    def staged_across_rows(value):
        end = {leaf: leaf + (-8 if leaf & 1 else 8) for leaf in range(leaves) if (leaf & 7) in (1, 6)}
        pairs = [(leaf, end.get(leaf, leaf)) for leaf in range(leaves)]
        return lax.ppermute(value, AXIS, [(a, b) for a, b in pairs if 0 <= b < leaves])

    def turned(value):
        pairs = [(leaf, (leaf & ~7) | ((leaf + (-2 if leaf & 1 else 2)) & 7)) for leaf in range(leaves)]
        return lax.ppermute(value, AXIS, pairs)

    def rows(count, dtype=BF16):
        return (count, 512), dtype

    def near_of(blocks, slots, total, name, after, cover=1):
        return near(near_mask, points, blocks, slots, total, name, after, cover)

    in_hbm = pl.BlockSpec(memory_space=pltpu.HBM)

    def kept_in_hbm(value):
        return pltpu.with_memory_space_constraint(value, pltpu.HBM)

    in_vmem = pl.BlockSpec(memory_space=pltpu.VMEM)
    (payload,) = call(
        pack_kernel,
        "pack",
        [rows(size + 128)],
        [kept_in_hbm(points), kept_in_hbm(weights)],
        0,
        scratch=[pltpu.SemaphoreType.DMA((6,))],
        in_specs=[in_hbm] * 2,
    )
    outer = moved(payload, -1, 1)
    partner = swap(payload, 1)
    send, keep = call(
        terms_kernel,
        "terms",
        [rows(1600), rows(1024, F32)],
        [payload, interp, skel_index, kept_in_hbm(transfers)],
        2 * 512 * 512 * (1024 + 5 * 512),
        scratch=[
            pltpu.VMEM((512, 512), BF16),
            pltpu.VMEM((5, 512, 512), BF16),
            pltpu.SemaphoreType.DMA((5,)),
        ],
        in_specs=[in_vmem, in_vmem, in_vmem, in_hbm],
    )
    came = swap(send, 1)
    total, token = near_of([payload], [None], None, "near_self", (send,), cover=20)

    to2, to4, to6, kept, pair = call(
        chip_kernel,
        "chip",
        [rows(448), rows(288), rows(288), rows(128, F32), rows(128)],
        [keep, came, send],
        1e6,
        after=(token, partner),
        scratch=[pltpu.VMEM((1024, 512), F32)],
    )
    from2, from4, from6 = swap(to2, 2), swap(to4, 4), swap(to6, 6)
    late, pair = lax.optimization_barrier((payload, pair))
    staged = staged_across_rows(late)
    total, token = near_of([partner, outer], [(2, 1), (1, 2)], total, "near_one", (pair,))

    to8, to16, ring = call(
        row_kernel,
        "row",
        [rows(128), rows(96), ((4, 64, 256), BF16)],
        [from2, from4, from6, kept, pair],
        1e8,
        after=(token,),
    )
    staged, outer, ring = lax.optimization_barrier((staged, outer, ring))
    second = turned(staged)
    past = swap(outer, 1)
    from8, from16, from24 = swap(to8, 8), swap(to16, 16), swap(to16, 24)
    coupled0, coupled1, coupled2 = call(
        couple_low_kernel,
        "couple_low",
        [rows(512), rows(256), rows(128)],
        [came, from2, from4, from6, pair, ring],
        1e6,
    )
    total, token = near_of([past], [(3, 0)], total, "near_past", (coupled2,), cover=0.01)
    part2, part4 = call(
        couple_high_kernel,
        "couple_high",
        [rows(256), rows(128)],
        [from8, from16, from24, to8, to16, coupled2],
        1e6,
        after=(token,),
    )
    back2, back4, back6 = swap(part2, 2), swap(part4, 4), swap(part4, 6)
    total, token = near_of([second], [(0, 3)], total, "near_second", (part4,))
    (mine,) = call(
        half_kernel, "half", [rows(1024)], [coupled1, part2, back2, back4, back6], 1e6, after=(token,)
    )
    theirs = swap(mine, 1)
    far, ready = call(
        far_kernel,
        "far",
        [rows(512, F32), ((size, 256), BF16)],
        [transfers, coupled0, mine, total, interp],
        2 * 512 * 512 * (512 + 4 * 256 + 512),
    )
    return call(
        product_kernel,
        "product",
        [((size, width), BF16)],
        [total, interp, transfers, far, theirs, ready],
        2 * 512 * 512 * (4 * 256 + 512),
        scratch=[pltpu.VMEM((size, width), BF16), pltpu.SemaphoreType.DMA((size // 128,))],
        out_space=pltpu.HBM,
    )[0]


def solution(mesh):
    return jax.shard_map(
        per_device,
        mesh=mesh,
        in_specs=(
            P(None, AXIS),
            P(AXIS, None),
            P(AXIS, None),
            P(AXIS, None, None, None),
            P(AXIS, None),
            P(AXIS, None),
        ),
        out_specs=P(AXIS, None),
        check_vma=False,
    )
```

```python
import math

import jax
import jax.numpy as jnp
from jax import lax
from jax.experimental import pallas as pl
from jax.experimental.pallas import tpu as pltpu
from jax.sharding import PartitionSpec as P

F32 = jnp.float32
BF16 = jnp.bfloat16
AXIS = "leaf"
VMEM_BYTES = 24 * 1024 * 1024
ROWS = 256
WORK = 1.0
LOW = 1.0


def dot(a, b, over=((1,), (0,))):
    return lax.dot_general(a, b, (over, ((), ())), preferred_element_type=F32)


def place():
    leaf = lax.axis_index(AXIS)
    return leaf & 1, (leaf >> 1) & 3, (leaf >> 3) & 3


def split_norm(wide, scale):
    norm = jnp.sum(wide * wide, axis=0, keepdims=True) * scale
    high = norm.astype(BF16).astype(F32)
    rest = norm - high
    middle = rest.astype(BF16).astype(F32)
    return high, middle, rest - middle


def lifted(points, left):
    dim, count = points.shape
    scale = math.log2(math.e) / dim
    wide = points.astype(F32)
    high, middle, low = split_norm(wide, -scale)
    row = lax.broadcasted_iota(jnp.int32, (16, count), 0)
    at = 0 if left else 3
    ones = 3 - at
    extra = jnp.where(row == at, high, jnp.where(row == at + 1, middle, jnp.where(row == at + 2, low, 0.0)))
    extra = jnp.where((row >= ones) & (row < ones + 3), 1.0, extra).astype(BF16)
    if left:
        scaled = wide * (2.0 * scale)
        first = scaled.astype(BF16)
        second = (scaled - first.astype(F32)).astype(BF16)
    else:
        first = second = points
    return jnp.concatenate([first, second, extra], axis=0)


def gaussian(left, right):
    return jnp.exp2(dot(left, right, ((0,), (0,)))).astype(BF16)


def call(body, name, outs, args, flops, smem=(), scratch=(), in_specs=None, after=(), out_space=pltpu.VMEM):
    specs = in_specs or [pl.BlockSpec(memory_space=pltpu.SMEM if k in smem else pltpu.VMEM) for k in range(len(args))]
    specs = specs + [pl.BlockSpec(memory_space=pl.ANY) for _ in after]
    taken = len(args)

    def reading(*refs):
        body(*refs[:taken], *refs[taken + len(after) :])

    moved = sum(a.size * a.dtype.itemsize for a in args) + sum(math.prod(s) * jnp.dtype(t).itemsize for s, t in outs)
    return pl.pallas_call(
        reading,
        name=name,
        in_specs=specs,
        out_specs=[pl.BlockSpec(memory_space=out_space) for _ in outs],
        out_shape=[jax.ShapeDtypeStruct(s, t) for s, t in outs],
        scratch_shapes=list(scratch),
        compiler_params=pltpu.CompilerParams(vmem_limit_bytes=VMEM_BYTES),
        cost_estimate=pl.CostEstimate(flops=int(flops * WORK), bytes_accessed=int(moved * WORK), transcendentals=0),
    )(*args, *after)


def pack(half):
    return jnp.concatenate([half[:32], half[32:]], axis=1)


def unpack(packed):
    return jnp.concatenate([packed[:, :256], packed[:, 256:]], axis=0)


def picked(columns, count, wide, kept):
    source = lax.broadcasted_iota(jnp.int32, (columns.shape[1], count), 0)
    target = lax.broadcasted_iota(jnp.int32, (columns.shape[1], count), 1)
    choice = (source == (target // kept) * wide + target % kept).astype(F32).astype(BF16)
    return dot(columns, choice).astype(BF16)


def start_all(copies):
    for copy in copies:
        copy.start()
    return copies


def wait_all(copies):
    for copy in copies:
        copy.wait()


def pack_kernel(points, weights, out, done):
    half = points.shape[1] // 2
    rows = weights.shape[0]
    quarter = rows // 4
    parts = [(weights.at[k * quarter : (k + 1) * quarter, :], out.at[k * quarter : (k + 1) * quarter, :]) for k in range(4)]
    parts += [(points.at[:, k * half : (k + 1) * half], out.at[rows + k * 64 : rows + k * 64 + 64, :]) for k in range(2)]
    wait_all(start_all([pltpu.make_async_copy(a, b, done.at[k]) for k, (a, b) in enumerate(parts)]))


def terms_kernel(w, p, index, transfers, send, keep, lifted_weights, t, done):
    core, _, _ = place()
    copies = start_all([pltpu.make_async_copy(transfers.at[0, (k + 1) % 5], t.at[k], done.at[k]) for k in range(5)])
    size = p.shape[0]
    lifted_weights[...] = dot(w[0:size, :], p[...], ((0,), (0,))).astype(BF16)
    rank = lax.broadcasted_iota(jnp.int32, (size // 2, index.shape[1]), 0)
    chosen = dot(w[size : size + 64, :], (rank == index[...]).astype(F32).astype(BF16))
    chosen = chosen + dot(w[size + 64 : size + 128, :], (rank + size // 2 == index[...]).astype(F32).astype(BF16))
    send[1536:1600, :] = chosen.astype(BF16)
    theirs = pl.multiple_of((1 - core) * 256, 256)
    mine = pl.multiple_of(core * 256, 256)
    for k in range(4):
        copies[k].wait()
        send[k * 256 : (k + 1) * 256, :] = dot(lifted_weights[pl.ds(theirs, 256), :], t[k]).astype(BF16)
        keep[k * 256 : (k + 1) * 256, :] = dot(lifted_weights[pl.ds(mine, 256), :], t[k])
    copies[4].wait()
    send[1024:1536, :] = dot(lifted_weights[...], t[4]).astype(BF16)


def chip_kernel(keep, came, sent, to2, to4, to6, kept, pair, total):
    core, x, _ = place()
    mine, theirs = sent[1536:1600, :], came[1536:1600, :]
    first = jnp.where(core == 0, mine, theirs)
    second = jnp.where(core == 0, theirs, mine)
    pair[0:64, :] = first
    pair[64:128, :] = second
    total[...] = keep[...] + came[0:1024, :].astype(F32)
    to2[192:448, :] = total[0:256, :].astype(BF16)
    to2[128:192, :] = jnp.concatenate([first[:, :256], second[:, :256]], axis=1)
    for level, at in ((3, 0), (4, 64)):
        for out, row, other in ((to2, 0, x ^ 1), (to4, 128, x ^ 2), (to6, 128, x ^ 3)):
            rows = pl.ds(pl.multiple_of((level - 1) * 256 + other * 64, 64), 64)
            out[row + at : row + at + 64, :] = total[rows, :].astype(BF16)
        kept[at : at + 64, :] = total[pl.ds(pl.multiple_of((level - 1) * 256 + x * 64, 64), 64), :]
    packed = pack(jnp.concatenate([first[:, :128], second[:, :128]], axis=1))
    for out, part in ((to4, x & 1), (to6, (x & 1) ^ 1)):
        out[0:128, :] = total[pl.ds(pl.multiple_of(256 + part * 128, 128), 128), :].astype(BF16)
        out[256:288, :] = packed


def row_kernel(from2, from4, from6, kept, pair, to8, to16, ring):
    _, x, _ = place()
    near = from2[128:192, :]
    ring[x] = jnp.concatenate([pair[0:64, 0:128], pair[64:128, 0:128]], axis=1)
    ring[x ^ 1] = jnp.concatenate([near[:, 0:128], near[:, 256:384]], axis=1)
    ring[x ^ 2] = unpack(from4[256:288, :])
    ring[x ^ 3] = unpack(from6[256:288, :])
    points3 = picked(jnp.concatenate([ring[k] for k in range(4)], axis=1), 512, 128, 64)
    for out, at in ((to8, 0), (to16, 64)):
        total = kept[at : at + 64, :] + from2[at : 64 + at, :].astype(F32)
        total = total + from4[128 + at : 192 + at, :].astype(F32) + from6[128 + at : 192 + at, :].astype(F32)
        out[0:64, :] = total.astype(BF16)
    to8[64:128, :] = points3
    to16[64:96, :] = pack(picked(points3, 256, 64, 32))


def couple(sums, own, sibling):
    return dot(sums, gaussian(lifted(sibling, True), lifted(own, False))).astype(BF16)


def couple_low_kernel(came, from2, from4, from6, pair, ring, out0, out1, out2):
    core, x, _ = place()
    first, second = pair[0:64, :], pair[64:128, :]
    out0[...] = couple(came[1024:1536, :], jnp.where(core == 0, first, second), jnp.where(core == 0, second, first))
    own = jnp.concatenate([first[:, 0:256], second[:, 0:256]], axis=1)
    out1[...] = couple(from2[192:448, :], own, from2[128:192, :])
    low = x & 2
    own = jnp.concatenate([ring[low], ring[low | 1]], axis=1)
    sibling = jnp.concatenate([ring[low ^ 2], ring[(low ^ 2) | 1]], axis=1)
    sums = (from4[0:128, :].astype(F32) + from6[0:128, :].astype(F32)).astype(BF16)
    out2[...] = couple(sums, own, sibling)


def couple_high_kernel(from8, from16, from24, to8, to16, coupled2, out2, out4):
    _, _, z = place()
    points3 = from8[64:128, :]
    level3 = couple(from8[0:64, :], to8[64:128, :], points3)
    mine, beside = unpack(to16[64:96, :]), picked(points3, 256, 64, 32)
    even = (z & 1) == 0
    own = jnp.concatenate([jnp.where(even, mine, beside), jnp.where(even, beside, mine)], axis=1)
    across, past = unpack(from16[64:96, :]), unpack(from24[64:96, :])
    sibling = jnp.concatenate([jnp.where(even, across, past), jnp.where(even, past, across)], axis=1)
    sums = (from16[0:64, :].astype(F32) + from24[0:64, :].astype(F32)).astype(BF16)
    level4 = couple(sums, own, sibling)
    out2[0:64, :] = level3
    out2[64:128, :] = level4
    out2[128:256, :] = coupled2[...]
    out4[0:64, :] = level3
    out4[64:128, :] = level4


def half_kernel(coupled1, own, from2, from4, from6, out):
    _, x, _ = place()
    out[0:256, :] = coupled1[...]
    out[pl.ds(pl.multiple_of(256 + (x & 1) * 128, 128), 128), :] = own[128:256, :]
    out[pl.ds(pl.multiple_of(256 + ((x & 1) ^ 1) * 128, 128), 128), :] = from2[128:256, :]
    for base, at in ((512, 0), (768, 64)):
        for part, block in ((x, own), (x ^ 1, from2), (x ^ 2, from4), (x ^ 3, from6)):
            out[pl.ds(pl.multiple_of(base + part * 64, 64), 64), :] = block[at : at + 64, :]


def near_kernel(count, slots, with_total, *refs):
    mask, own = refs[0], refs[1]
    blocks = refs[2 : 2 + count]
    total = refs[2 + count] if with_total else None
    out, token = refs[-2], refs[-1]
    token[...] = jnp.zeros_like(token)
    core, _, _ = place()
    size = own.shape[1]
    left = lifted(own[...], True)
    result = [None] * (size // ROWS)
    for block, slot in zip(blocks, slots):
        if slot is None:
            right = lifted(own[...], False)
        else:
            columns = jnp.concatenate([block[size : size + 64, :], block[size + 64 : size + 128, :]], axis=1)
            right = lifted(columns, False)
            flag = jnp.where(core == 0, mask[0, slot[0]], mask[0, slot[1]]).astype(F32)
        values = block[0:size, :]
        for k in range(size // ROWS):
            tile = gaussian(left[:, k * ROWS : (k + 1) * ROWS], right)
            part = dot(tile, values)
            if slot is not None:
                part = part * flag
            result[k] = part if result[k] is None else result[k] + part
    for k in range(size // ROWS):
        rows = slice(k * ROWS, (k + 1) * ROWS)
        out[rows, :] = result[k] + total[rows, :] if with_total else result[k]


def near(mask, points, blocks, slots, total, name, after, cover=1):
    args = [mask, points, *blocks] + ([] if total is None else [total])
    size, width = points.shape[1], blocks[0].shape[1]

    def body(*refs):
        near_kernel(len(blocks), slots, total is not None, *refs)

    flops = cover * 2 * len(blocks) * size * size * (width + 256)
    return call(body, name, [((size, width), F32), ((8, 128), F32)], args, flops, smem=(0,), after=after)


def columns_of(core):
    return pl.ds(pl.multiple_of(core * 256, 256), 256)


def with_levels(value, transfers, half):
    for level in range(1, 5):
        value = value + dot(transfers[0, level], half[(level - 1) * 256 : level * 256, :], ((1,), (1,)))
    return value


def far_kernel(transfers, coupled0, mine, total, interp, begun, out):
    core, _, _ = place()
    begun[...] = dot(transfers[0, 0], coupled0[...], ((1,), (1,)))
    columns = columns_of(core)
    skeleton = with_levels(begun[:, columns], transfers, mine).astype(BF16)
    block = total.shape[0] // 2
    for k in range(2):
        rows = slice(k * block, (k + 1) * block)
        out[rows, :] = (total[rows, columns] + dot(interp[rows, :], skeleton)).astype(BF16)


def product_kernel(total, interp, transfers, begun, theirs, ready, product, out, done):
    core, _, _ = place()
    columns = columns_of(1 - core)
    block = total.shape[0] // 4
    blocks = [slice(k * block, (k + 1) * block) for k in range(4)]
    copies = start_all(
        [
            pltpu.make_async_copy(ready.at[rows, :], product.at[rows, columns_of(core)], done.at[k])
            for k, rows in enumerate(blocks)
        ]
    )
    skeleton = with_levels(begun[:, columns], transfers, theirs).astype(BF16)
    for k, rows in enumerate(blocks):
        out[rows, :] = (total[rows, columns] + dot(interp[rows, :], skeleton)).astype(BF16)
        copies += start_all([pltpu.make_async_copy(out.at[rows, :], product.at[rows, columns], done.at[4 + k])])
    wait_all(copies)


def per_device(points, weights, interp, transfers, near_mask, skel_index):
    leaves = lax.axis_size(AXIS)
    size, width = weights.shape

    def swap(value, mask):
        return lax.ppermute(value, AXIS, [(leaf, leaf ^ mask) for leaf in range(leaves)])

    def moved(value, even, odd):
        pairs = [(leaf, leaf + (odd if leaf & 1 else even)) for leaf in range(leaves)]
        return lax.ppermute(value, AXIS, [(a, b) for a, b in pairs if 0 <= b < leaves])

    def staged_across_rows(value):
        end = {leaf: leaf + (-8 if leaf & 1 else 8) for leaf in range(leaves) if (leaf & 7) in (1, 6)}
        pairs = [(leaf, end.get(leaf, leaf)) for leaf in range(leaves)]
        return lax.ppermute(value, AXIS, [(a, b) for a, b in pairs if 0 <= b < leaves])

    def turned(value):
        pairs = [(leaf, (leaf & ~7) | ((leaf + (-2 if leaf & 1 else 2)) & 7)) for leaf in range(leaves)]
        return lax.ppermute(value, AXIS, pairs)

    def rows(count, dtype=BF16):
        return (count, 512), dtype

    def near_of(blocks, slots, total, name, after, cover=1):
        return near(near_mask, points, blocks, slots, total, name, after, cover)

    in_hbm = pl.BlockSpec(memory_space=pltpu.HBM)

    def kept_in_hbm(value):
        return pltpu.with_memory_space_constraint(value, pltpu.HBM)

    in_vmem = pl.BlockSpec(memory_space=pltpu.VMEM)
    (payload,) = call(
        pack_kernel,
        "pack",
        [rows(size + 128)],
        [kept_in_hbm(points), kept_in_hbm(weights)],
        0,
        scratch=[pltpu.SemaphoreType.DMA((6,))],
        in_specs=[in_hbm] * 2,
    )
    outer = moved(payload, -1, 1)
    partner = swap(payload, 1)
    send, keep = call(
        terms_kernel,
        "terms",
        [rows(1600), rows(1024, F32)],
        [payload, interp, skel_index, kept_in_hbm(transfers)],
        2 * 512 * 512 * (1024 + 5 * 512),
        scratch=[
            pltpu.VMEM((512, 512), BF16),
            pltpu.VMEM((5, 512, 512), BF16),
            pltpu.SemaphoreType.DMA((5,)),
        ],
        in_specs=[in_vmem, in_vmem, in_vmem, in_hbm],
    )
    came = swap(send, 1)
    total, token = near_of([payload], [None], None, "near_self", (send,), cover=20)

    to2, to4, to6, kept, pair = call(
        chip_kernel,
        "chip",
        [rows(448), rows(288), rows(288), rows(128, F32), rows(128)],
        [keep, came, send],
        1e6,
        after=(token, partner),
        scratch=[pltpu.VMEM((1024, 512), F32)],
    )
    from2, from4, from6 = swap(to2, 2), swap(to4, 4), swap(to6, 6)
    late, pair = lax.optimization_barrier((payload, pair))
    staged = staged_across_rows(late)
    total, token = near_of([partner, outer], [(2, 1), (1, 2)], total, "near_one", (pair,))

    to8, to16, ring = call(
        row_kernel,
        "row",
        [rows(128), rows(96), ((4, 64, 256), BF16)],
        [from2, from4, from6, kept, pair],
        1e8,
        after=(token,),
    )
    staged, outer, ring = lax.optimization_barrier((staged, outer, ring))
    second = turned(staged)
    past = swap(outer, 1)
    from8, from16, from24 = swap(to8, 8), swap(to16, 16), swap(to16, 24)
    coupled0, coupled1, coupled2 = call(
        couple_low_kernel,
        "couple_low",
        [rows(512), rows(256), rows(128)],
        [came, from2, from4, from6, pair, ring],
        1e6,
    )
    total, token = near_of([past], [(3, 0)], total, "near_past", (coupled2,), cover=0.01)
    part2, part4 = call(
        couple_high_kernel,
        "couple_high",
        [rows(256), rows(128)],
        [from8, from16, from24, to8, to16, coupled2],
        1e6,
        after=(token,),
    )
    back2, back4, back6 = swap(part2, 2), swap(part4, 4), swap(part4, 6)
    total, token = near_of([second], [(0, 3)], total, "near_second", (part4,))
    (mine,) = call(
        half_kernel, "half", [rows(1024)], [coupled1, part2, back2, back4, back6], 1e6, after=(token,)
    )
    theirs = swap(mine, 1)
    far, ready = call(
        far_kernel,
        "far",
        [rows(512, F32), ((size, 256), BF16)],
        [transfers, coupled0, mine, total, interp],
        2 * 512 * 512 * (512 + 4 * 256 + 512),
    )
    return call(
        product_kernel,
        "product",
        [((size, width), BF16)],
        [total, interp, transfers, far, theirs, ready],
        2 * 512 * 512 * (4 * 256 + 512),
        scratch=[pltpu.VMEM((size, 256), BF16), pltpu.SemaphoreType.DMA((8,))],
        out_space=pltpu.HBM,
    )[0]


def solution(mesh):
    return jax.shard_map(
        per_device,
        mesh=mesh,
        in_specs=(
            P(None, AXIS),
            P(AXIS, None),
            P(AXIS, None),
            P(AXIS, None, None, None),
            P(AXIS, None),
            P(AXIS, None),
        ),
        out_specs=P(AXIS, None),
        check_vma=False,
    )
```
